128 devices in a mesh: lat: 8 (over z_hi, y), lon: 16 (over x, z_lo, core).
Axes of the slice: x: 4, y: 4, z: 4 (z_hi: 2, z_lo: 2; z = z_hi * 2 + z_lo), core: 2. Of those that a mesh axis runs over, the one named last changes fastest.
Arguments:
- queries: bfloat16 [128, 256, 1024], P(('lat', 'lon')), may hold values from -32 to 32
- keys: bfloat16 [128, 256, 1024], P(('lat', 'lon')), may hold values from -32 to 32
- values: bfloat16 [128, 256, 1024], P(('lat', 'lon')), may hold values from -6 to 6
- grads_out: bfloat16 [128, 256, 1024], P(('lat', 'lon')), may hold values from -6 to 6
Outputs:
- grad_queries: bfloat16 [128, 256, 1024], P('lat', 'lon')
- grad_keys: bfloat16 [128, 256, 1024], P('lat', 'lon')
- grad_values: bfloat16 [128, 256, 1024], P('lat', 'lon')
The draws below stay inside these ranges and needn't reach their ends.
All inputs are finite; a program needn't handle non-finite values.
Results may differ from the reference program's by a relative error of at most 0.02.
Values may be sent and summed in bfloat16 or wider, within the bound.
A program may use at most 448 MiB of HBM per device.

```python
import jax
import jax.numpy as jnp
from jax import lax

HEADS = 16
RADIUS = 6
TILE = 8
D = 1024
NLAT = 128
NLON = 256


def draw_queries(key, part):
    key = jax.random.fold_in(key, 1)
    drawn = jnp.clip(jax.random.normal(key, (NLAT, NLON, D), jnp.float32), -6.0, 6.0)
    return drawn.astype(jnp.bfloat16)


def draw_keys(key, part):
    key = jax.random.fold_in(key, 2)
    drawn = jnp.clip(jax.random.normal(key, (NLAT, NLON, D), jnp.float32), -6.0, 6.0)
    return drawn.astype(jnp.bfloat16)


def shard_levels(key, extent, split, smallest, high):
    def one(position, blocks):
        draws = jax.random.uniform(jax.random.fold_in(jax.random.fold_in(key, 6), position), (blocks,), jnp.float32, smallest / len(split), high / len(split))
        return jnp.repeat(jnp.exp(draws), extent[position] // blocks).reshape((-1,) + (1,) * (len(extent) - position - 1))

    gain = one(*split[0])
    for cut in split[1:]:
        gain = gain * one(*cut)
    return gain


def normal_values(own_key, shape, deviation, most, cuts=(), dtype=jnp.bfloat16):
    entries = deviation * jax.random.normal(own_key, shape, jnp.float32)
    if cuts:
        entries = entries * shard_levels(own_key, shape, cuts, -0.22, 0.18)
    return jnp.clip(entries, -most, most).astype(dtype)


def setup_inputs(seed: int = 0) -> dict:
    splits = jax.random.split(jax.random.key(seed), 5)
    queries = draw_queries(jax.random.fold_in(splits[4], 71), 0)
    keys = draw_keys(jax.random.fold_in(splits[4], 71), 0)
    values = normal_values(splits[2], (NLAT, NLON, D), 1.0, 6.0, ((0, 128),))
    grads_out = normal_values(splits[3], (NLAT, NLON, D), 1.0, 6.0, ((0, 128),))
    return dict(queries=queries, keys=keys, values=values, grads_out=grads_out)


masked_score = -1e30


def window_grads(queries, grads_out, keys, values, key_first, total_rows):
    query_rows, query_cols, features = queries.shape
    tile_cols = query_cols // TILE
    tile_rows = query_rows // TILE
    head_size = features // HEADS
    score_scale = head_size ** -0.5
    offsets = jnp.arange(3 * TILE)[None, :] - jnp.arange(TILE)[:, None]
    inside = (offsets >= 0) & (offsets <= 2 * RADIUS)
    allowed = inside[:, None, :, None] & inside[None, :, None, :]

    def one_row(index, carry):
        grad_q, grad_kv = carry
        first_row = (index * TILE).astype(jnp.int32)
        q_tile = lax.dynamic_slice_in_dim(queries, first_row, TILE, 0).reshape(TILE, tile_cols, TILE, HEADS, head_size)
        d_tile = lax.dynamic_slice_in_dim(grads_out, first_row, TILE, 0).reshape(TILE, tile_cols, TILE, HEADS, head_size)
        k_rows = lax.dynamic_slice_in_dim(keys, first_row, 3 * TILE, 0).reshape(3 * TILE, tile_cols + 2, TILE, HEADS, head_size)
        v_rows = lax.dynamic_slice_in_dim(values, first_row, 3 * TILE, 0).reshape(3 * TILE, tile_cols + 2, TILE, HEADS, head_size)
        k_win = jnp.concatenate([k_rows[:, 0:tile_cols], k_rows[:, 1:tile_cols + 1], k_rows[:, 2:tile_cols + 2]], axis=2)
        v_win = jnp.concatenate([v_rows[:, 0:tile_cols], v_rows[:, 1:tile_cols + 1], v_rows[:, 2:tile_cols + 2]], axis=2)
        global_rows = key_first + first_row + jnp.arange(3 * TILE)
        row_ok = (global_rows >= 0) & (global_rows < total_rows)
        valid = allowed & row_ok[None, None, :, None]
        q32 = q_tile.astype(jnp.float32)
        d32 = d_tile.astype(jnp.float32)
        scores = jnp.einsum("acbhe,icjhe->chabij", q32, k_win.astype(jnp.float32)) * score_scale
        scores = jnp.where(valid, scores, masked_score)
        top_score = jnp.max(scores, axis=(4, 5), keepdims=True)
        weights = jnp.exp(scores - top_score)
        probs = weights / jnp.sum(weights, axis=(4, 5), keepdims=True)
        probs_low = probs.astype(jnp.bfloat16)
        d_probs = jnp.einsum("acbhe,icjhe->chabij", d32, v_win.astype(jnp.float32))
        centre = jnp.sum(probs * d_probs, axis=(4, 5), keepdims=True)
        d_scores = (probs * (d_probs - centre) * score_scale).astype(jnp.bfloat16)
        ds32 = d_scores.astype(jnp.float32)
        dq_tile = jnp.einsum("chabij,icjhe->acbhe", ds32, k_win.astype(jnp.float32))
        grad_q = lax.dynamic_update_slice_in_dim(grad_q, dq_tile.reshape(TILE, query_cols, features).astype(jnp.bfloat16), first_row, 0)
        dk_win = jnp.einsum("chabij,acbhe->icjhe", ds32, q32)
        dv_win = jnp.einsum("chabij,acbhe->icjhe", probs_low.astype(jnp.float32), d32)
        both = jnp.stack([dk_win, dv_win]).reshape(2, 3 * TILE, tile_cols, 3, TILE, HEADS, head_size)
        plain = ((0, 0), (0, 0))
        rest = ((0, 0), (0, 0), (0, 0))
        folded = jnp.pad(both[:, :, :, 0], plain + ((0, 2),) + rest)
        folded = folded + jnp.pad(both[:, :, :, 1], plain + ((1, 1),) + rest)
        folded = folded + jnp.pad(both[:, :, :, 2], plain + ((2, 0),) + rest)
        folded = folded.reshape(2, 3 * TILE, query_cols + 2 * TILE, features)
        current = lax.dynamic_slice_in_dim(grad_kv, first_row, 3 * TILE, 1)
        grad_kv = lax.dynamic_update_slice_in_dim(grad_kv, current + folded, first_row, 1)
        return grad_q, grad_kv

    begin = (jnp.zeros((query_rows, query_cols, features), jnp.bfloat16),
             jnp.zeros((2, query_rows + 2 * TILE, query_cols + 2 * TILE, features), jnp.float32))
    return lax.fori_loop(0, tile_rows, one_row, begin)


def extend(field):
    spare_cells = 2 * TILE - 2 * RADIUS
    wrapped = jnp.concatenate([field[:, NLON - RADIUS:], field, field[:, :RADIUS]], axis=1)
    return jnp.pad(wrapped, ((RADIUS, RADIUS + spare_cells), (0, spare_cells), (0, 0)))


def reference(queries, keys, values, grads_out):
    grad_q, grad_kv = window_grads(queries, grads_out, extend(keys), extend(values), -RADIUS, NLAT)
    middle = grad_kv[:, RADIUS:RADIUS + NLAT]
    core = middle[:, :, RADIUS:RADIUS + NLON]
    core = core.at[:, :, NLON - RADIUS:].add(middle[:, :, :RADIUS])
    core = core.at[:, :, :RADIUS].add(middle[:, :, NLON + RADIUS:NLON + 2 * RADIUS])
    return grad_q, core[0].astype(jnp.bfloat16), core[1].astype(jnp.bfloat16)
```

```python
import jax
import jax.numpy as jnp
from jax import lax
from jax.experimental import pallas as pl
from jax.experimental.pallas import tpu as pltpu
from jax.sharding import PartitionSpec as P

RADIUS = 6
SIDE = 8
HEAD = 64
LANES = 128

masked_score = -1e30


def dot(a, b, ca, cb):
    return lax.dot_general(a, b, (((ca,), (cb,)), ((), ())), preferred_element_type=jnp.float32)


def window_mask(lat, lats, half, rows, cols):
    half_rows = rows // 2
    wide = cols + 2 * SIDE
    span = half_rows + 2 * RADIUS
    shape = (span * wide, half_rows * cols)
    key = lax.broadcasted_iota(jnp.int32, shape, 0)
    query = lax.broadcasted_iota(jnp.int32, shape, 1)
    down = key // wide - query // cols
    right = key % wide - query % cols
    row = lat * rows - RADIUS + half * half_rows + key // wide
    ok = (down >= 0) & (down <= 2 * RADIUS)
    ok &= (right >= SIDE - RADIUS) & (right <= SIDE + RADIUS)
    ok &= (row >= 0) & (row < lats * rows)
    ok = jnp.where(ok, 0.0, masked_score)
    return jnp.concatenate([ok, ok], axis=1)


def pair_grads(q, d, k, v, mask):
    lane = lax.broadcasted_iota(jnp.int32, q.shape, 1)
    first = lane < HEAD
    zero = jnp.zeros_like(q)
    q2 = jnp.concatenate([jnp.where(first, q, zero), jnp.where(first, zero, q)], axis=0)
    d2 = jnp.concatenate([jnp.where(first, d, zero), jnp.where(first, zero, d)], axis=0)
    s = dot(k, q2, 1, 1) * (HEAD ** -0.5) + mask
    top = jnp.max(s, axis=0, keepdims=True)
    e = jnp.exp(s - top)
    r = 1.0 / jnp.sum(e, axis=0, keepdims=True)
    p = e * r
    dp = dot(v, d2, 1, 1)
    centre = jnp.sum(p * dp, axis=0, keepdims=True)
    ds = (p * (dp - centre) * (HEAD ** -0.5)).astype(jnp.bfloat16)
    dv = dot(p.astype(jnp.bfloat16), d2, 1, 0)
    dk = dot(ds, q2, 1, 0)
    dq = dot(ds, k, 0, 0)
    count = q.shape[0]
    dq = jnp.where(first, dq[:count], dq[count:])
    return dq, dk, dv


def grads_kernel(lats, lat_ref, own_ref, up_ref, down_ref, dq_ref, mid_ref, upg_ref, downg_ref, mask_ref, total_ref):
    rows, cols = 16, 16
    wide = cols + 2 * SIDE

    @pl.when(pl.program_id(0) == 0)
    def _():
        for half in range(2):
            mask_ref[half] = window_mask(lat_ref[0], lats, half, rows, cols)

    q = own_ref[:, 0:cols, :].reshape(rows * cols, LANES)
    d = own_ref[:, cols:2 * cols, :].reshape(rows * cols, LANES)
    base = 2 * cols

    def keys_of(start):
        parts = [r[:, a + start:a + start + wide, :].reshape(-1, LANES) for r, a in ((up_ref, 0), (own_ref, base), (down_ref, 0))]
        return jnp.concatenate(parts, axis=0)

    k = keys_of(0)
    v = keys_of(wide)
    count = rows * cols // 2
    span = (rows // 2 + 2 * RADIUS) * wide
    shift = (rows // 2) * wide
    for half in range(2):
        here = slice(half * count, (half + 1) * count)
        there = slice(half * shift, half * shift + span)
        dq, dk, dv = pair_grads(q[here], d[here], k[there], v[there], mask_ref[half])
        dq_ref[here, :] = dq.astype(dq_ref.dtype)
        if half == 0:
            total_ref[0, 0:span] = dk
            total_ref[1, 0:span] = dv
        else:
            lap = span - shift
            total_ref[0, shift:span] += dk[:lap]
            total_ref[1, shift:span] += dv[:lap]
            total_ref[0, span:] = dk[lap:]
            total_ref[1, span:] = dv[lap:]
    edge = RADIUS * wide
    total = total_ref[...]
    upg_ref[...] = total[:, :edge].astype(jnp.bfloat16)
    downg_ref[...] = total[:, -edge:].astype(jnp.bfloat16)
    mid_ref[...] = total[:, edge:-edge]


def window_grads(own, up, down, lats):
    rows, cols = 16, 16
    wide = cols + 2 * SIDE
    features = own.shape[-1]
    lat = lax.axis_index("lat").astype(jnp.int32).reshape(1)
    keys = (rows + 2 * RADIUS) * wide
    span = (rows // 2 + 2 * RADIUS) * wide

    def block(shape):
        lead = (0,) * (len(shape) - 1)
        return pl.BlockSpec(shape[:-1] + (LANES,), lambda g: lead + (g,))

    import functools
    outs = [((rows * cols, features), jnp.bfloat16), ((2, rows * wide, features), jnp.float32),
            ((2, RADIUS * wide, features), jnp.bfloat16), ((2, RADIUS * wide, features), jnp.bfloat16)]
    return pl.pallas_call(
        functools.partial(grads_kernel, lats),
        grid=(features // LANES,),
        in_specs=[pl.BlockSpec(memory_space=pltpu.SMEM), block(own.shape), block(up.shape), block(down.shape)],
        out_specs=[block(s) for s, _ in outs],
        out_shape=[jax.ShapeDtypeStruct(s, t) for s, t in outs],
        scratch_shapes=[pltpu.VMEM((2, span, rows * cols), jnp.float32), pltpu.VMEM((2, keys, LANES), jnp.float32)],
        compiler_params=pltpu.CompilerParams(vmem_limit_bytes=48 * 1024 * 1024),
    )(lat, own, up, down)


def on_device(queries, keys, values, grads_out):
    lats, lons = lax.axis_size("lat"), lax.axis_size("lon")
    queries, keys, values, grads_out = (a[0] for a in (queries, keys, values, grads_out))
    features = queries.shape[-1]
    cols = queries.shape[0] // lons
    rows = lons
    wide = cols + 2 * SIDE

    def plain(a):
        return a.reshape(lons, cols, features)

    def extended(a):
        b = plain(a)
        left = jnp.roll(b, 1, axis=0)[:, cols - SIDE:]
        right = jnp.roll(b, -1, axis=0)[:, :SIDE]
        return jnp.concatenate([left, b, right], axis=1)

    chunks = jnp.concatenate([plain(queries), plain(grads_out), extended(keys), extended(values)], axis=1)
    own = lax.all_to_all(chunks, "lon", split_axis=0, concat_axis=0, tiled=True)
    higher = [(i, i + 1) for i in range(lats - 1)]
    lower = [(i + 1, i) for i in range(lats - 1)]
    kv = own[:, 2 * cols:]
    up = lax.ppermute(kv[rows - RADIUS:], "lat", higher)
    down = lax.ppermute(kv[:RADIUS], "lat", lower)
    dq, mid, up_grad, down_grad = window_grads(own, up, down, lats)
    from_low = lax.ppermute(down_grad, "lat", higher)
    from_high = lax.ppermute(up_grad, "lat", lower)
    f32 = jnp.float32
    edge = RADIUS * wide
    mid = jnp.concatenate([mid[:, :edge] + from_low.astype(f32), mid[:, edge:-edge], mid[:, -edge:] + from_high.astype(f32)], axis=1)
    mid = mid.reshape(2, rows, wide, features)
    right = [(i, (i + 1) % lons) for i in range(lons)]
    left = [((i + 1) % lons, i) for i in range(lons)]
    from_left = lax.ppermute(mid[:, :, wide - SIDE:].astype(jnp.bfloat16), "lon", right)
    from_right = lax.ppermute(mid[:, :, :SIDE].astype(jnp.bfloat16), "lon", left)
    core = mid[:, :, SIDE:SIDE + cols] + jnp.concatenate([from_left, from_right], axis=2).astype(f32)
    core = core.astype(jnp.bfloat16)
    return dq.reshape(rows, cols, features), core[0], core[1]


def solution(mesh):
    placed = P(("lat", "lon"), None, None)
    return jax.shard_map(
        on_device,
        mesh=mesh,
        in_specs=(placed,) * 4,
        out_specs=(P("lat", "lon", None),) * 3,
        check_vma=False,
    )
```

```python
import functools
import itertools

import jax
import jax.numpy as jnp
from jax import lax
from jax.experimental import pallas as pl
from jax.experimental.pallas import tpu as pltpu
from jax.sharding import PartitionSpec as P

HEAD = 64
LANES = 128
RADIUS = 6
SIDE = 8
ROWS = 16
TILE = 16
COLS = 2 * TILE
WIDE = COLS + 2 * SIDE
TALL = ROWS + 2 * RADIUS
HALF = ROWS // 2
SPAN = HALF + 2 * RADIUS
TWIDE = TILE + 2 * SIDE
BLOCKS = 4
CHIPS = 8
SPREAD = 15

MESH = pl.DeviceIdType.MESH
bf16 = jnp.bfloat16
f32 = jnp.float32
masked_score = -1e30


def dot(a, b, ca, cb):
    return lax.dot_general(a, b, (((ca,), (cb,)), ((), ())), preferred_element_type=f32)


def window_mask(lat, lats, half):
    shape = (SPAN * TWIDE, HALF * TILE)
    key = lax.broadcasted_iota(jnp.int32, shape, 0)
    query = lax.broadcasted_iota(jnp.int32, shape, 1)
    down = key // TWIDE - query // TILE
    right = key % TWIDE - query % TILE
    row = lat * ROWS - RADIUS + half * HALF + key // TWIDE
    ok = (down >= 0) & (down <= 2 * RADIUS)
    ok &= (right >= SIDE - RADIUS) & (right <= SIDE + RADIUS)
    ok &= (row >= 0) & (row < lats * ROWS)
    ok = jnp.where(ok, 0.0, masked_score)
    return jnp.concatenate([ok, ok], axis=1)


def pair_grads(q, d, k, v, mask):
    first = lax.broadcasted_iota(jnp.int32, q.shape, 1) < HEAD
    zero = jnp.zeros_like(q)
    q = q * (HEAD ** -0.5)
    q2 = jnp.concatenate([jnp.where(first, q, zero), jnp.where(first, zero, q)], axis=0)
    d2 = jnp.concatenate([jnp.where(first, d, zero), jnp.where(first, zero, d)], axis=0)
    s = dot(k, q2, 1, 1) + mask
    e = jnp.exp(s - jnp.max(s, axis=0, keepdims=True))
    p = e * (1.0 / jnp.sum(e, axis=0, keepdims=True))
    dp = dot(v, d2, 1, 1)
    centre = jnp.sum(p * dp, axis=0, keepdims=True)
    ds = (p * (dp - centre)).astype(bf16)
    dv = dot(p.astype(bf16), d2, 1, 0)
    dk = dot(ds, q2, 1, 0)
    dq = dot(ds, k, 0, 0) * (HEAD ** -0.5)
    count = q.shape[0]
    return jnp.where(first, dq[:count], dq[count:]), dk, dv


STEPS = [(1, 0, 0), (3, 0, 0), (0, 1, 0), (2, 0, 0), (1, 1, 0), (3, 1, 0), (0, 1, 1), (2, 1, 0), (1, 0, 1),
         (3, 0, 1), (2, 0, 1), (1, 1, 1), (3, 1, 1), (2, 1, 1), (0, 0, 1)]


def kernel(lats, q_ref, k_ref, v_ref, d_ref, out_ref, send_kv, send_qd, got_kv, got_qd, mask, acc, edge_out, edge_in,
           side_out, side_in, final, sent_kv, sent_qd, came_kv, came_qd, own_sem, relay_out, relay_in, lat_out, lat_in,
           lon_out, lon_in, swap_out, swap_in, keep_sem):
    lat, lon = lax.axis_index("lat"), lax.axis_index("lon")
    x, z, core = lon // 4, (lon // 2) % 2, lon % 2
    chip = lon // 2
    partner = (lat, 2 * chip + 1 - core)
    left = (lat, 2 * ((chip + CHIPS - 1) % CHIPS) + core)
    right = (lat, 2 * ((chip + 1) % CHIPS) + core)
    above, below = (lat - 1, lon), (lat + 1, lon)
    has_above, has_below = lat > 0, lat < lats - 1

    def other(step):
        return lat, (((x + step[0]) % 4) * 2 + (z + step[1]) % 2) * 2 + (core + step[2]) % 2

    barrier = pltpu.get_barrier_semaphore()
    for step in STEPS:
        pl.semaphore_signal(barrier, inc=1, device_id=other(step), device_id_type=MESH)

    @pl.when(has_above)
    def _():
        pl.semaphore_signal(barrier, inc=1, device_id=above, device_id_type=MESH)

    @pl.when(has_below)
    def _():
        pl.semaphore_signal(barrier, inc=1, device_id=below, device_id_type=MESH)

    def prepare(b):
        for c in range(2):
            lanes = pl.ds(pl.multiple_of(c * BLOCKS * LANES + b * LANES, LANES), LANES)
            for i, ref in enumerate((k_ref, v_ref)):
                a = ref[0, :, lanes].astype(f32)
                a = jnp.concatenate([a[-SIDE:], a, a[:SIDE]], axis=0).astype(bf16)
                for m in range(CHIPS):
                    send_kv[b, 2 * m + c, i * WIDE:(i + 1) * WIDE] = a[m * COLS:m * COLS + WIDE]
            for i, ref in enumerate((q_ref, d_ref)):
                for m in range(CHIPS):
                    send_qd[b, 2 * m + c, i * COLS:(i + 1) * COLS] = ref[0, m * COLS:(m + 1) * COLS, lanes]

    def spread(b):
        for out, into, gone, came, row, i in ((send_kv, got_kv, sent_kv, came_kv, lon + RADIUS, 0),
                                              (send_qd, got_qd, sent_qd, came_qd, lon, 1)):
            for step in STEPS:
                to = other(step)
                pltpu.make_async_remote_copy(out.at[b, to[1]], into.at[b, row], gone.at[b], came.at[b],
                                             device_id=to, device_id_type=MESH).start()
            pltpu.make_async_copy(out.at[b, lon], into.at[b, row], own_sem.at[b, i]).start()

    def own_wait(b, out, into, row, i):
        pltpu.make_async_copy(out.at[b, lon], into.at[b, row], own_sem.at[b, i]).wait()

    def all_wait(ref, sem, b):
        pltpu.make_async_copy(ref.at[b, 0:SPREAD], ref.at[b, 0:SPREAD], sem.at[b]).wait()

    prepare(0)
    peers = SPREAD + (lat + lats - 1) // lats + (2 * lats - 2 - lat) // lats
    pl.semaphore_wait(barrier, peers)

    @pl.loop(0, BLOCKS)
    def _(b):
        spread(b)

        @pl.when(b < BLOCKS - 1)
        def _():
            prepare(b + 1)

    for half in range(2):
        mask[half] = window_mask(lat, lats, half)

    @pl.when(lat == 0)
    def _():
        for b in range(BLOCKS):
            got_kv[b, 0:RADIUS] = jnp.zeros((RADIUS, 2 * WIDE, LANES), bf16)

    @pl.when(lat == lats - 1)
    def _():
        for b in range(BLOCKS):
            got_kv[b, TALL - RADIUS:TALL] = jnp.zeros((RADIUS, 2 * WIDE, LANES), bf16)

    def relay_up(b):
        return pltpu.make_async_remote_copy(got_kv.at[b, RADIUS:2 * RADIUS], got_kv.at[b, TALL - RADIUS:TALL], relay_out.at[b, 0],
                                            relay_in.at[b, 0], device_id=above, device_id_type=MESH)

    def relay_down(b):
        return pltpu.make_async_remote_copy(got_kv.at[b, ROWS:ROWS + RADIUS], got_kv.at[b, 0:RADIUS], relay_out.at[b, 1],
                                            relay_in.at[b, 1], device_id=below, device_id_type=MESH)

    def edge_up(b):
        return pltpu.make_async_remote_copy(edge_out.at[b, 0], edge_in.at[b, 0], lat_out.at[b, 0], lat_in.at[b, 0],
                                            device_id=above, device_id_type=MESH)

    def edge_down(b):
        return pltpu.make_async_remote_copy(edge_out.at[b, 1], edge_in.at[b, 1], lat_out.at[b, 1], lat_in.at[b, 1],
                                            device_id=below, device_id_type=MESH)

    def side_left(b):
        return pltpu.make_async_remote_copy(side_out.at[b, 0], side_in.at[b, 0], lon_out.at[b, 0], lon_in.at[b, 0],
                                            device_id=left, device_id_type=MESH)

    def side_right(b):
        return pltpu.make_async_remote_copy(side_out.at[b, 1], side_in.at[b, 1], lon_out.at[b, 1], lon_in.at[b, 1],
                                            device_id=right, device_id_type=MESH)

    out_lanes = lambda b: pl.ds(pl.multiple_of(core * BLOCKS * LANES + b * LANES, LANES), LANES)

    def swap(b):
        return pltpu.make_async_remote_copy(final.at[b, 1 - core], out_ref.at[:, :, :, out_lanes(b)], swap_out.at[b], swap_in.at[b],
                                            device_id=partner, device_id_type=MESH)

    def keep(b):
        return pltpu.make_async_copy(final.at[b, core], out_ref.at[:, :, :, out_lanes(b)], keep_sem.at[b])

    def pass_keys(b):
        own_wait(b, send_kv, got_kv, lon + RADIUS, 0)
        all_wait(got_kv, came_kv, b)

        @pl.when(has_above)
        def _():
            relay_up(b).start()

        @pl.when(has_below)
        def _():
            relay_down(b).start()

    def compute(b):
        own_wait(b, send_qd, got_qd, lon, 1)
        all_wait(got_qd, came_qd, b)
        acc[b] = jnp.zeros((2, TALL, WIDE, LANES), f32)

        def tiles(half):
            @pl.loop(0, 2)
            def _(t):
                rows = slice(half * HALF, (half + 1) * HALF)
                spans = slice(half * HALF, half * HALF + SPAN)
                at = lambda start, size: pl.ds(pl.multiple_of(start + t * TILE, TILE), size)
                q = got_qd[b, rows, at(0, TILE)].reshape(HALF * TILE, LANES)
                d = got_qd[b, rows, at(COLS, TILE)].reshape(HALF * TILE, LANES)
                k = got_kv[b, spans, at(0, TWIDE)].reshape(SPAN * TWIDE, LANES)
                v = got_kv[b, spans, at(WIDE, TWIDE)].reshape(SPAN * TWIDE, LANES)
                dq, dk, dv = pair_grads(q, d, k, v, mask[half])
                final[b, t, 0, rows] = dq.astype(bf16).reshape(HALF, TILE, LANES)
                acc[b, 0, spans, at(0, TWIDE)] += dk.reshape(SPAN, TWIDE, LANES)
                acc[b, 1, spans, at(0, TWIDE)] += dv.reshape(SPAN, TWIDE, LANES)

        @pl.when(has_above)
        def _():
            relay_down(b).wait_recv()

        tiles(0)

        @pl.when(has_above)
        def _():
            edge_out[b, 0] = acc[b, :, 0:RADIUS].astype(bf16)
            edge_up(b).start()

        @pl.when(has_below)
        def _():
            relay_up(b).wait_recv()

        tiles(1)

        @pl.when(has_below)
        def _():
            edge_out[b, 1] = acc[b, :, TALL - RADIUS:TALL].astype(bf16)
            edge_down(b).start()

    def add_edges(b):
        @pl.when(has_below)
        def _():
            edge_up(b).wait_recv()
            acc[b, :, ROWS:ROWS + RADIUS] += edge_in[b, 0].astype(f32)

        @pl.when(has_above)
        def _():
            edge_down(b).wait_recv()
            acc[b, :, RADIUS:2 * RADIUS] += edge_in[b, 1].astype(f32)

        own = slice(RADIUS, RADIUS + ROWS)
        side_out[b, 0] = jnp.concatenate([acc[b, 0, own, 0:SIDE], acc[b, 1, own, 0:SIDE]], axis=1).astype(bf16)
        side_out[b, 1] = jnp.concatenate([acc[b, 0, own, WIDE - SIDE:WIDE], acc[b, 1, own, WIDE - SIDE:WIDE]], axis=1).astype(bf16)
        side_left(b).start()
        side_right(b).start()

    def add_sides(b):
        own = slice(RADIUS, RADIUS + ROWS)
        side_left(b).wait_recv()
        side_right(b).wait_recv()
        from_right = side_in[b, 0].astype(f32)
        from_left = side_in[b, 1].astype(f32)
        for i in range(2):
            whole = acc[b, i, own, SIDE:SIDE + COLS]
            part = slice(i * SIDE, (i + 1) * SIDE)
            whole = jnp.concatenate([whole[:, :SIDE] + from_left[:, part], whole[:, SIDE:COLS - SIDE],
                                     whole[:, COLS - SIDE:] + from_right[:, part]], axis=1).astype(bf16)
            final[b, 0, 1 + i] = whole[:, :TILE]
            final[b, 1, 1 + i] = whole[:, TILE:]
        swap(b).start()
        keep(b).start()

    @pl.loop(0, BLOCKS + 2)
    def _(i):
        @pl.when(i < BLOCKS)
        def _():
            pass_keys(i)

        @pl.when(i >= 2)
        def _():
            add_sides(i - 2)

        @pl.when((i >= 1) & (i < BLOCKS + 1))
        def _():
            add_edges(i - 1)

        @pl.when(i < BLOCKS)
        def _():
            compute(i)

    @pl.loop(0, BLOCKS)
    def _(b):
        all_wait(got_kv, sent_kv, b)
        all_wait(got_qd, sent_qd, b)
        side_left(b).wait_send()
        side_right(b).wait_send()

        @pl.when(has_above)
        def _():
            relay_up(b).wait_send()
            edge_up(b).wait_send()

        @pl.when(has_below)
        def _():
            relay_down(b).wait_send()
            edge_down(b).wait_send()

        keep(b).wait()
        swap(b).wait()


def on_device(queries, keys, values, grads_out):
    lats = lax.axis_size("lat")
    features = queries.shape[-1]
    vmem = lambda *shape: pltpu.VMEM(shape, bf16)
    sems = lambda *shape: pltpu.SemaphoreType.DMA(shape)
    lons = 2 * CHIPS
    out = pl.pallas_call(
        functools.partial(kernel, lats),
        out_shape=jax.ShapeDtypeStruct((3, ROWS, TILE, features), bf16),
        in_specs=[pl.BlockSpec(memory_space=pltpu.VMEM)] * 4,
        out_specs=pl.BlockSpec(memory_space=pl.ANY),
        scratch_shapes=[
            vmem(BLOCKS, lons, 2 * WIDE, LANES),
            vmem(BLOCKS, lons, 2 * COLS, LANES),
            vmem(BLOCKS, TALL, 2 * WIDE, LANES),
            vmem(BLOCKS, ROWS, 2 * COLS, LANES),
            pltpu.VMEM((2, SPAN * TWIDE, 2 * HALF * TILE), f32),
            pltpu.VMEM((BLOCKS, 2, TALL, WIDE, LANES), f32),
            vmem(BLOCKS, 2, 2, RADIUS, WIDE, LANES),
            vmem(BLOCKS, 2, 2, RADIUS, WIDE, LANES),
            vmem(BLOCKS, 2, ROWS, 2 * SIDE, LANES),
            vmem(BLOCKS, 2, ROWS, 2 * SIDE, LANES),
            vmem(BLOCKS, 2, 3, ROWS, TILE, LANES),
            sems(BLOCKS), sems(BLOCKS), sems(BLOCKS), sems(BLOCKS),
            sems(BLOCKS, 2), sems(BLOCKS, 2), sems(BLOCKS, 2), sems(BLOCKS, 2), sems(BLOCKS, 2),
            sems(BLOCKS, 2), sems(BLOCKS, 2), sems(BLOCKS), sems(BLOCKS), sems(BLOCKS),
        ],
        compiler_params=pltpu.CompilerParams(collective_id=0, has_side_effects=True, vmem_limit_bytes=56 * 1024 * 1024),
    )(queries, keys, values, grads_out)
    return out[0], out[1], out[2]


def solution(mesh):
    placed = P(("lat", "lon"), None, None)
    return jax.shard_map(
        on_device,
        mesh=mesh,
        in_specs=(placed,) * 4,
        out_specs=(P("lat", "lon", None),) * 3,
        check_vma=False,
    )
```

```python
import functools

import jax
import jax.numpy as jnp
from jax import lax
from jax.experimental import pallas as pl
from jax.experimental.pallas import tpu as pltpu
from jax.sharding import PartitionSpec as P

HEAD = 64
LANES = 128
RADIUS = 6
SIDE = 8
LON = 256
ROWS = 16
TILE = 16
TILES = 8
STAGES = 4
STEP = 2 * TILE
COLS = TILES * TILE
WIDE = COLS + 2 * SIDE
TALL = ROWS + 2 * RADIUS
HALF = ROWS // 2
SPAN = HALF + 2 * RADIUS
TWIDE = TILE + 2 * SIDE
DEVICES = 16
OTHERS = DEVICES - 1

MESH = pl.DeviceIdType.MESH
bf16 = jnp.bfloat16
f32 = jnp.float32
masked_score = -1e30


def dot(a, b, ca, cb):
    return lax.dot_general(a, b, (((ca,), (cb,)), ((), ())), preferred_element_type=f32)


def window_mask(lat, lats, half):
    shape = (SPAN * TWIDE, HALF * TILE)
    key = lax.broadcasted_iota(jnp.int32, shape, 0)
    query = lax.broadcasted_iota(jnp.int32, shape, 1)
    down = key // TWIDE - query // TILE
    right = key % TWIDE - query % TILE
    row = lat * ROWS - RADIUS + half * HALF + key // TWIDE
    ok = (down >= 0) & (down <= 2 * RADIUS)
    ok &= (right >= SIDE - RADIUS) & (right <= SIDE + RADIUS)
    ok &= (row >= 0) & (row < lats * ROWS)
    ok = jnp.where(ok, 0.0, masked_score)
    return jnp.concatenate([ok, ok], axis=1)


def pair_grads(q, d, k, v, mask):
    first = lax.broadcasted_iota(jnp.int32, q.shape, 1) < HEAD
    zero = jnp.zeros_like(q)
    q = q * (HEAD ** -0.5)
    q2 = jnp.concatenate([jnp.where(first, q, zero), jnp.where(first, zero, q)], axis=0)
    d2 = jnp.concatenate([jnp.where(first, d, zero), jnp.where(first, zero, d)], axis=0)
    s = dot(k, q2, 1, 1) + mask
    e = jnp.exp(s - jnp.max(s, axis=0, keepdims=True))
    p = e * (1.0 / jnp.sum(e, axis=0, keepdims=True))
    dp = dot(v, d2, 1, 1)
    centre = jnp.sum(p * dp, axis=0, keepdims=True)
    ds = (p * (dp - centre)).astype(bf16)
    dv = dot(p.astype(bf16), d2, 1, 0)
    dk = dot(ds, q2, 1, 0)
    dq = dot(ds, k, 0, 0) * (HEAD ** -0.5)
    count = q.shape[0]
    return jnp.where(first, dq[:count], dq[count:]), dk, dv


HOPS = [(1, 0, 0), (3, 0, 0), (0, 1, 0), (2, 0, 0), (1, 1, 0), (3, 1, 0), (0, 1, 1), (2, 1, 0), (1, 0, 1),
        (3, 0, 1), (2, 0, 1), (1, 1, 1), (3, 1, 1), (2, 1, 1), (0, 0, 1)]


def either(core, a, b):
    return (1 - core) * a + core * b


def by(value, unit):
    return pl.multiple_of(value, unit)


def kernel(lats, q_ref, k_ref, v_ref, d_ref, out_ref, raw, shifted, send_qd, got_kv, got_qd, mask, acc, edge_out, edge_in,
           last_out, last_in, side_out, side_in, final_q, final_kv, load_sem, sent_kv, sent_qd, came_kv, came_qd, own_sem,
           relay_out, relay_in, lat_out, lat_in, side_gone, side_came, q_gone, q_came, kv_gone, kv_came):
    lat, lon = lax.axis_index("lat"), lax.axis_index("lon")
    x, z, core = lon // 4, (lon // 2) % 2, lon % 2
    deep = lats // 2
    group = 2 * x + (z + lat // deep) % 2
    partner = (lat, lon + 1 - 2 * core)
    has_above, has_below = lat > 0, lat < lats - 1
    more_above, more_below = (lat + lats - 1) // lats, (2 * lats - 2 - lat) // lats

    def neighbour(other_lat):
        return other_lat, 4 * x + 2 * ((z + lat // deep + other_lat // deep) % 2) + core

    above, below = neighbour(lat - more_above), neighbour(lat + more_below)

    def start_block(g, c):
        return (2 * g + (DEVICES // 2) * c) % DEVICES

    def other(hop):
        ox, oz, oc = (x + hop[0]) % 4, (z + hop[1]) % 2, (core + hop[2]) % 2
        return 4 * ox + 2 * oz + oc, 2 * ox + (oz + lat // deep) % 2, oc

    loads = [pltpu.make_async_copy(r.at[0], t, load_sem.at[i]) for i, (r, t) in enumerate(
        ((k_ref, raw.at[0]), (v_ref, raw.at[1]), (q_ref, send_qd.at[0]), (d_ref, send_qd.at[1])))]
    for load in loads:
        load.start()

    barrier = pltpu.get_barrier_semaphore()
    for hop in HOPS:
        pl.semaphore_signal(barrier, inc=1, device_id=(lat, other(hop)[0]), device_id_type=MESH)

    @pl.when(has_above)
    def _():
        pl.semaphore_signal(barrier, inc=1, device_id=above, device_id_type=MESH)

    @pl.when(has_below)
    def _():
        pl.semaphore_signal(barrier, inc=1, device_id=below, device_id_type=MESH)

    def kv_at(u, c):
        return either(c, 16 + STEP * u, 96 - STEP * u)

    def q_at(u, c):
        return either(c, STEP * u, 96 - STEP * u)

    def done_at(u):
        return by(either(core, STEP * u, 112 - STEP * u), TILE)

    def tile_of(i):
        return either(core, i, TILES - 1 - i)

    for i in range(2):
        loads[i].wait()
        for g in range(8):
            lanes = slice(g * LANES, (g + 1) * LANES)
            a = raw[i, :, lanes].astype(f32)
            a = jnp.concatenate([a[-SIDE:], a, a[:STEP - SIDE]], axis=0)
            shifted[i, :, lanes] = a.astype(bf16)
    loads[2].wait()
    loads[3].wait()

    pl.semaphore_wait(barrier, OTHERS + more_above + more_below)

    def kv_copy(u, g, c, first):
        off = either(c, 0, 96) if first else kv_at(u, c)
        size = 3 * TILE if first else STEP
        begin = (TILE * start_block(g, c) + off) % LON
        src = shifted.at[:, pl.ds(by(begin, TILE), size), pl.ds(by(g * LANES, LANES), LANES)]
        return src, got_kv.at[:, lon + RADIUS, pl.ds(by(off, TILE), size), :]

    def qd_copy(u, g, c):
        off = q_at(u, c)
        begin = (TILE * start_block(g, c) + off) % LON
        src = send_qd.at[:, pl.ds(by(begin, TILE), STEP), pl.ds(by(g * LANES, LANES), LANES)]
        return src, got_qd.at[:, lon, pl.ds(by(off, TILE), STEP), :]

    def spread(u, first=False):
        for kind in range(2):
            gone, came = ((sent_kv, came_kv), (sent_qd, came_qd))[kind]
            for hop in HOPS:
                to, g, c = other(hop)
                src, dst = qd_copy(u, g, c) if kind else kv_copy(u, g, c, first)
                pltpu.make_async_remote_copy(src, dst, gone.at[u], came.at[u], device_id=(lat, to), device_id_type=MESH).start()
            src, dst = qd_copy(u, group, core) if kind else kv_copy(u, group, core, first)
            pltpu.make_async_copy(src, dst, own_sem.at[u, kind]).start()

    spread(0, True)

    @pl.loop(1, STAGES)
    def _(u):
        spread(u)

    for half in range(2):
        mask[half] = window_mask(lat, lats, half)

    @pl.loop(0, TALL)
    def _(row):
        acc[:, row] = jnp.zeros((2, WIDE, LANES), f32)

    @pl.when(lat == 0)
    def _():
        got_kv[:, 0:RADIUS] = jnp.zeros((2, RADIUS, WIDE, LANES), bf16)

    @pl.when(lat == lats - 1)
    def _():
        got_kv[:, TALL - RADIUS:TALL] = jnp.zeros((2, RADIUS, WIDE, LANES), bf16)

    def came_wait(sem, u, ref, size):
        blank = ref.at[:, 0:OTHERS, 0:size, :]
        pltpu.make_async_copy(blank, blank, sem.at[u]).wait()

    def own_wait(u, kind, ref, size):
        blank = ref.at[:, 0, 0:size, :]
        pltpu.make_async_copy(blank, blank, own_sem.at[u, kind]).wait()

    def relay(u, way, first):
        off = either(core, 0, 96) if first else kv_at(u, core)
        cols = pl.ds(by(off, TILE), 3 * TILE if first else STEP)
        here, there, to = ((slice(RADIUS, 2 * RADIUS), slice(TALL - RADIUS, TALL), above),
                           (slice(ROWS, ROWS + RADIUS), slice(0, RADIUS), below))[way]
        return pltpu.make_async_remote_copy(got_kv.at[:, here, cols, :], got_kv.at[:, there, cols, :], relay_out.at[u, way],
                                            relay_in.at[u, way], device_id=to, device_id_type=MESH)

    def edge(u, way):
        return pltpu.make_async_remote_copy(edge_out.at[u, way], edge_in.at[u, way], lat_out.at[u, way], lat_in.at[u, way],
                                            device_id=(above, below)[way], device_id_type=MESH)

    def last_edge(way):
        return pltpu.make_async_remote_copy(last_out.at[way], last_in.at[way], lat_out.at[STAGES, way], lat_in.at[STAGES, way],
                                            device_id=(above, below)[way], device_id_type=MESH)

    def side(i):
        return pltpu.make_async_remote_copy(side_out.at[i], side_in.at[i], side_gone.at[i], side_came.at[i],
                                            device_id=partner, device_id_type=MESH)

    out_lanes = pl.ds(by(group * LANES, LANES), LANES)

    def owner(i):
        return (start_block(group, core) + tile_of(i)) % DEVICES

    def q_pair(i):
        return final_q.at[i], out_ref.at[0, :, :, out_lanes]

    def kv_pair(i):
        return final_kv.at[i], out_ref.at[1:3, :, :, out_lanes]

    def hand_out(pair, i, gone, came):
        src, dst = pair(i)
        to = owner(i)

        @pl.when(to == lon)
        def _():
            pltpu.make_async_copy(src, dst, came.at[group]).start()

        @pl.when(to != lon)
        def _():
            pltpu.make_async_remote_copy(src, dst, gone.at[i], came.at[group], device_id=(lat, to), device_id_type=MESH).start()

    def hand_out_wait(pair, i, gone):
        src, dst = pair(i)
        to = owner(i)

        @pl.when(to != lon)
        def _():
            pltpu.make_async_remote_copy(src, dst, gone.at[i], gone.at[i], device_id=(lat, to), device_id_type=MESH).wait_send()

    own = slice(RADIUS, RADIUS + ROWS)

    def hand_out_kv(i):
        at = pl.ds(by(SIDE + TILE * tile_of(i), SIDE), TILE)
        final_kv[i] = acc[:, own, at].astype(bf16)
        hand_out(kv_pair, i, kv_gone, kv_came)

    def on_ways(make, then):
        @pl.when(has_above)
        def _():
            then(make(0))

        @pl.when(has_below)
        def _():
            then(make(1))

    def pass_keys(u):
        def go(first):
            size = 3 * TILE if first else STEP
            own_wait(u, 0, got_kv, size)
            came_wait(came_kv, u, got_kv, size)
            on_ways(lambda way: relay(u, way, first), lambda copy: copy.start())

        @pl.when(u == 0)
        def _():
            go(True)

        @pl.when(u > 0)
        def _():
            go(False)

    def relay_wait(u, way):
        @pl.when(u == 0)
        def _():
            relay(u, way, True).wait_recv()

        @pl.when(u > 0)
        def _():
            relay(u, way, False).wait_recv()

    def compute(u):
        own_wait(u, 1, got_qd, STEP)
        came_wait(came_qd, u, got_qd, STEP)

        def tiles(half):
            @pl.loop(0, 2)
            def _(j):
                i = 2 * u + j
                begin = by(tile_of(i) * TILE, TILE)
                rows = slice(half * HALF, (half + 1) * HALF)
                spans = slice(half * HALF, half * HALF + SPAN)
                at, near = pl.ds(begin, TILE), pl.ds(begin, TWIDE)
                q = got_qd[0, rows, at].reshape(HALF * TILE, LANES)
                d = got_qd[1, rows, at].reshape(HALF * TILE, LANES)
                k = got_kv[0, spans, near].reshape(SPAN * TWIDE, LANES)
                v = got_kv[1, spans, near].reshape(SPAN * TWIDE, LANES)
                dq, dk, dv = pair_grads(q, d, k, v, mask[half])
                final_q[i, rows] = dq.astype(bf16).reshape(HALF, TILE, LANES)
                acc[0, spans, near] += dk.reshape(SPAN, TWIDE, LANES)
                acc[1, spans, near] += dv.reshape(SPAN, TWIDE, LANES)

        last = by((1 - core) * COLS, TILE)

        def send_edge(way):
            rows = (slice(0, RADIUS), slice(TALL - RADIUS, TALL))[way]
            edge_out[u, way] = acc[:, rows, pl.ds(done_at(u), STEP)].astype(bf16)
            edge(u, way).start()

            @pl.when(u == STAGES - 1)
            def _():
                last_out[way] = acc[:, rows, pl.ds(last, TILE)].astype(bf16)
                last_edge(way).start()

        @pl.when(has_above)
        def _():
            relay_wait(u, 1)

        tiles(0)

        @pl.when(has_above)
        def _():
            send_edge(0)

        @pl.when(has_below)
        def _():
            relay_wait(u, 0)

        tiles(1)

        @pl.when(has_below)
        def _():
            send_edge(1)

        hand_out(q_pair, 2 * u, q_gone, q_came)
        hand_out(q_pair, 2 * u + 1, q_gone, q_came)

    def add_edges(u):
        last = by((1 - core) * COLS, TILE)

        def add(way):
            rows = (slice(ROWS, ROWS + RADIUS), slice(RADIUS, 2 * RADIUS))[way]
            edge(u, way).wait_recv()
            acc[:, rows, pl.ds(done_at(u), STEP)] += edge_in[u, way].astype(f32)

            @pl.when(u == STAGES - 1)
            def _():
                last_edge(way).wait_recv()
                acc[:, rows, pl.ds(last, TILE)] += last_in[way].astype(f32)

        @pl.when(has_below)
        def _():
            add(0)

        @pl.when(has_above)
        def _():
            add(1)

        def send_side(i, at):
            cols = pl.ds(by(at, SIDE), SIDE)
            side_out[i] = jnp.concatenate([acc[0, own, cols], acc[1, own, cols]], axis=1).astype(bf16)
            side(i).start()

        @pl.when(u == 0)
        def _():
            send_side(0, core * (WIDE - SIDE))

        @pl.when(u == STAGES - 1)
        def _():
            send_side(1, (1 - core) * (WIDE - SIDE))

        @pl.when(u > 0)
        def _():
            hand_out_kv(2 * u - 1)
            hand_out_kv(2 * u)

    def add_side(i, at, tile):
        side(i).wait_recv()
        cols = pl.ds(by(at, SIDE), SIDE)
        got = side_in[i].astype(f32)
        acc[0, own, cols] += got[:, :SIDE]
        acc[1, own, cols] += got[:, SIDE:]
        hand_out_kv(tile)

    @pl.loop(0, STAGES + 1)
    def _(i):
        @pl.when(i < STAGES)
        def _():
            pass_keys(i)

        @pl.when(i == 2)
        def _():
            add_side(0, either(core, SIDE, COLS), 0)

        @pl.when(i > 0)
        def _():
            add_edges(i - 1)

        @pl.when(i < STAGES)
        def _():
            compute(i)

    add_side(1, either(core, COLS, SIDE), TILES - 1)

    came_wait(sent_kv, 0, got_kv, 3 * TILE)
    came_wait(sent_qd, 0, got_qd, STEP)
    on_ways(lambda way: relay(0, way, True), lambda copy: copy.wait_send())
    on_ways(lambda way: edge(0, way), lambda copy: copy.wait_send())

    @pl.loop(1, STAGES)
    def _(u):
        came_wait(sent_kv, u, got_kv, STEP)
        came_wait(sent_qd, u, got_qd, STEP)
        on_ways(lambda way: relay(u, way, False), lambda copy: copy.wait_send())
        on_ways(lambda way: edge(u, way), lambda copy: copy.wait_send())

    on_ways(last_edge, lambda copy: copy.wait_send())
    side(0).wait_send()
    side(1).wait_send()

    @pl.loop(0, TILES)
    def _(i):
        hand_out_wait(q_pair, i, q_gone)
        hand_out_wait(kv_pair, i, kv_gone)
        for pair, came in ((q_pair, q_came), (kv_pair, kv_came)):
            src, dst = pair(i)
            pltpu.make_async_copy(src, dst, came.at[i]).wait()


def on_device(queries, keys, values, grads_out):
    lats = lax.axis_size("lat")
    features = queries.shape[-1]
    vmem = lambda *shape: pltpu.VMEM(shape, bf16)
    sems = lambda *shape: pltpu.SemaphoreType.DMA(shape)
    out = pl.pallas_call(
        functools.partial(kernel, lats),
        out_shape=jax.ShapeDtypeStruct((3, ROWS, TILE, features), bf16),
        in_specs=[pl.BlockSpec(memory_space=pl.ANY)] * 4,
        out_specs=pl.BlockSpec(memory_space=pl.ANY),
        scratch_shapes=[
            vmem(2, LON, features),
            vmem(2, LON + STEP, features),
            vmem(2, LON, features),
            vmem(2, TALL, WIDE, LANES),
            vmem(2, ROWS, COLS, LANES),
            pltpu.VMEM((2, SPAN * TWIDE, 2 * HALF * TILE), f32),
            pltpu.VMEM((2, TALL, WIDE, LANES), f32),
            vmem(STAGES, 2, 2, RADIUS, STEP, LANES),
            vmem(STAGES, 2, 2, RADIUS, STEP, LANES),
            vmem(2, 2, RADIUS, TILE, LANES),
            vmem(2, 2, RADIUS, TILE, LANES),
            vmem(2, ROWS, 2 * SIDE, LANES),
            vmem(2, ROWS, 2 * SIDE, LANES),
            vmem(TILES, ROWS, TILE, LANES),
            vmem(TILES, 2, ROWS, TILE, LANES),
            sems(4), sems(STAGES), sems(STAGES), sems(STAGES), sems(STAGES), sems(STAGES, 2),
            sems(STAGES, 2), sems(STAGES, 2), sems(STAGES + 1, 2), sems(STAGES + 1, 2), sems(2), sems(2),
            sems(TILES), sems(TILES), sems(TILES), sems(TILES),
        ],
        compiler_params=pltpu.CompilerParams(collective_id=0, has_side_effects=True, vmem_limit_bytes=56 * 1024 * 1024),
    )(queries, keys, values, grads_out)
    return out[0], out[1], out[2]


def solution(mesh):
    placed = P(("lat", "lon"), None, None)
    return jax.shard_map(
        on_device,
        mesh=mesh,
        in_specs=(placed,) * 4,
        out_specs=(P("lat", "lon", None),) * 3,
        check_vma=False,
    )
```

```python
import functools

import jax
import jax.numpy as jnp
from jax import lax
from jax.experimental import pallas as pl
from jax.experimental.pallas import tpu as pltpu
from jax.sharding import PartitionSpec as P

HEAD = 64
LANES = 128
RADIUS = 6
SIDE = 8
LON = 256
ROWS = 16
TILE = 16
TILES = 8
PARTS = 4
STEP = 2 * TILE
COLS = TILES * TILE
WIDE = COLS + 2 * SIDE
TALL = ROWS + 2 * RADIUS
HALF = ROWS // 2
SPAN = HALF + 2 * RADIUS
TWIDE = TILE + 2 * SIDE
DEVICES = 16
OTHERS = DEVICES - 1

MESH = pl.DeviceIdType.MESH
bf16 = jnp.bfloat16
f32 = jnp.float32
masked_score = -1e30


def dot(a, b, ca, cb):
    return lax.dot_general(a, b, (((ca,), (cb,)), ((), ())), preferred_element_type=f32)


def window_mask(lat, lats, half):
    shape = (SPAN * TWIDE, HALF * TILE)
    key = lax.broadcasted_iota(jnp.int32, shape, 0)
    query = lax.broadcasted_iota(jnp.int32, shape, 1)
    down = key // TWIDE - query // TILE
    right = key % TWIDE - query % TILE
    row = lat * ROWS - RADIUS + half * HALF + key // TWIDE
    ok = (down >= 0) & (down <= 2 * RADIUS)
    ok &= (right >= SIDE - RADIUS) & (right <= SIDE + RADIUS)
    ok &= (row >= 0) & (row < lats * ROWS)
    ok = jnp.where(ok, 0.0, masked_score)
    return jnp.concatenate([ok, ok], axis=1)


def pair_grads(q, d, k, v, mask):
    first = lax.broadcasted_iota(jnp.int32, q.shape, 1) < HEAD
    zero = jnp.zeros_like(q)
    q = q * (HEAD ** -0.5)
    q2 = jnp.concatenate([jnp.where(first, q, zero), jnp.where(first, zero, q)], axis=0)
    d2 = jnp.concatenate([jnp.where(first, d, zero), jnp.where(first, zero, d)], axis=0)
    s = dot(k, q2, 1, 1) + mask
    e = jnp.exp(s - jnp.max(s, axis=0, keepdims=True))
    p = e * (1.0 / jnp.sum(e, axis=0, keepdims=True))
    dp = dot(v, d2, 1, 1)
    centre = jnp.sum(p * dp, axis=0, keepdims=True)
    ds = (p * (dp - centre)).astype(bf16)
    dv = dot(p.astype(bf16), d2, 1, 0)
    dk = dot(ds, q2, 1, 0)
    dq = dot(ds, k, 0, 0) * (HEAD ** -0.5)
    count = q.shape[0]
    return jnp.where(first, dq[:count], dq[count:]), dk, dv


HOPS = [(1, 0, 0), (3, 0, 0), (0, 1, 0), (2, 0, 0), (1, 1, 0), (3, 1, 0), (0, 1, 1), (2, 1, 0), (1, 0, 1),
        (3, 0, 1), (2, 0, 1), (1, 1, 1), (3, 1, 1), (2, 1, 1), (0, 0, 1)]


def either(core, a, b):
    return (1 - core) * a + core * b


def by(value, unit):
    return pl.multiple_of(value, unit)


def kernel(lats, q_ref, k_ref, v_ref, d_ref, out_ref, raw, shifted, send_qd, got_kv, got_qd, mask, acc, edge_out, edge_in,
           last_out, last_in, side_out, side_in, final_q, final_kv, load_sem, sent_kv, sent_qd, came_kv, came_qd, own_kv, own_qd,
           relay_out, relay_in, lat_out, lat_in, side_gone, side_came, q_gone, q_came, kv_gone, kv_came):
    lat, lon = lax.axis_index("lat"), lax.axis_index("lon")
    x, z, core = lon // 4, (lon // 2) % 2, lon % 2
    deep = lats // 2
    group = 2 * x + (z + lat // deep) % 2
    partner = (lat, lon + 1 - 2 * core)
    has_above, has_below = lat > 0, lat < lats - 1
    more_above, more_below = (lat + lats - 1) // lats, (2 * lats - 2 - lat) // lats

    def neighbour(other_lat):
        return other_lat, 4 * x + 2 * ((z + lat // deep + other_lat // deep) % 2) + core

    above, below = neighbour(lat - more_above), neighbour(lat + more_below)

    def start_block(g, c):
        return (2 * g + (DEVICES // 2) * c) % DEVICES

    def other(hop):
        ox, oz, oc = (x + hop[0]) % 4, (z + hop[1]) % 2, (core + hop[2]) % 2
        return 4 * ox + 2 * oz + oc, 2 * ox + (oz + lat // deep) % 2, oc

    loads = [pltpu.make_async_copy(r.at[0], t, load_sem.at[i]) for i, (r, t) in enumerate(
        ((k_ref, raw.at[0]), (v_ref, raw.at[1]), (q_ref, send_qd.at[0]), (d_ref, send_qd.at[1])))]
    for load in loads:
        load.start()

    barrier = pltpu.get_barrier_semaphore()
    for hop in HOPS:
        pl.semaphore_signal(barrier, inc=1, device_id=(lat, other(hop)[0]), device_id_type=MESH)

    @pl.when(has_above)
    def _():
        pl.semaphore_signal(barrier, inc=1, device_id=above, device_id_type=MESH)

    @pl.when(has_below)
    def _():
        pl.semaphore_signal(barrier, inc=1, device_id=below, device_id_type=MESH)

    def kv_at(u, c):
        return either(c, 16 + STEP * u, 96 - STEP * u)

    def done_at(i):
        return by(either(core, TILE * i, COLS - TILE * i), TILE)

    def tile_of(i, c):
        return either(c, i, TILES - 1 - i)

    for i in range(2):
        loads[i].wait()
        for g in range(8):
            lanes = slice(g * LANES, (g + 1) * LANES)
            a = raw[i, :, lanes].astype(f32)
            a = jnp.concatenate([a[-SIDE:], a, a[:STEP - SIDE]], axis=0)
            shifted[i, :, lanes] = a.astype(bf16)
    loads[2].wait()
    loads[3].wait()

    pl.semaphore_wait(barrier, OTHERS + more_above + more_below)

    def kv_copy(u, g, c, first):
        off = either(c, 0, 96) if first else kv_at(u, c)
        size = 3 * TILE if first else STEP
        begin = (TILE * start_block(g, c) + off) % LON
        src = shifted.at[:, pl.ds(by(begin, TILE), size), pl.ds(by(g * LANES, LANES), LANES)]
        return src, got_kv.at[:, lon + RADIUS, pl.ds(by(off, TILE), size), :]

    def qd_copy(i, g, c):
        off = TILE * tile_of(i, c)
        begin = (TILE * start_block(g, c) + off) % LON
        src = send_qd.at[:, pl.ds(by(begin, TILE), TILE), pl.ds(by(g * LANES, LANES), LANES)]
        return src, got_qd.at[:, lon, pl.ds(by(off, TILE), TILE), :]

    def spread(pair, i, gone, came, own_sem):
        for hop in HOPS:
            to, g, c = other(hop)
            src, dst = pair(i, g, c)
            pltpu.make_async_remote_copy(src, dst, gone.at[i], came.at[i], device_id=(lat, to), device_id_type=MESH).start()
        src, dst = pair(i, group, core)
        pltpu.make_async_copy(src, dst, own_sem.at[i]).start()

    def spread_kv(u, first=False):
        spread(lambda i, g, c: kv_copy(i, g, c, first), u, sent_kv, came_kv, own_kv)

    def spread_qd(i):
        spread(qd_copy, i, sent_qd, came_qd, own_qd)

    spread_kv(0, True)
    spread_qd(0)

    @pl.loop(1, PARTS)
    def _(u):
        spread_kv(u)

        @pl.loop(2 * u - 1, 2 * u + 1)
        def _(i):
            spread_qd(i)

    spread_qd(TILES - 1)

    for half in range(2):
        mask[half] = window_mask(lat, lats, half)

    @pl.loop(0, TALL)
    def _(row):
        acc[:, row] = jnp.zeros((2, WIDE, LANES), f32)

    @pl.when(lat == 0)
    def _():
        got_kv[:, 0:RADIUS] = jnp.zeros((2, RADIUS, WIDE, LANES), bf16)

    @pl.when(lat == lats - 1)
    def _():
        got_kv[:, TALL - RADIUS:TALL] = jnp.zeros((2, RADIUS, WIDE, LANES), bf16)

    def came_wait(sem, u, ref, size):
        blank = ref.at[:, 0:OTHERS, 0:size, :]
        pltpu.make_async_copy(blank, blank, sem.at[u]).wait()

    def own_wait(sem, u, ref, size):
        blank = ref.at[:, 0, 0:size, :]
        pltpu.make_async_copy(blank, blank, sem.at[u]).wait()

    def relay(u, way, first):
        off = either(core, 0, 96) if first else kv_at(u, core)
        cols = pl.ds(by(off, TILE), 3 * TILE if first else STEP)
        here, there, to = ((slice(RADIUS, 2 * RADIUS), slice(TALL - RADIUS, TALL), above),
                           (slice(ROWS, ROWS + RADIUS), slice(0, RADIUS), below))[way]
        return pltpu.make_async_remote_copy(got_kv.at[:, here, cols, :], got_kv.at[:, there, cols, :], relay_out.at[u, way],
                                            relay_in.at[u, way], device_id=to, device_id_type=MESH)

    def edge(u, way):
        return pltpu.make_async_remote_copy(edge_out.at[u, way], edge_in.at[u, way], lat_out.at[u, way], lat_in.at[u, way],
                                            device_id=(above, below)[way], device_id_type=MESH)

    def last_edge(way):
        return pltpu.make_async_remote_copy(last_out.at[way], last_in.at[way], lat_out.at[TILES, way], lat_in.at[TILES, way],
                                            device_id=(above, below)[way], device_id_type=MESH)

    def side(i):
        return pltpu.make_async_remote_copy(side_out.at[i], side_in.at[i], side_gone.at[i], side_came.at[i],
                                            device_id=partner, device_id_type=MESH)

    out_lanes = pl.ds(by(group * LANES, LANES), LANES)

    def owner(i):
        return (start_block(group, core) + tile_of(i, core)) % DEVICES

    def q_pair(i):
        return final_q.at[i], out_ref.at[0, :, :, out_lanes]

    def kv_pair(i):
        return final_kv.at[i], out_ref.at[1:3, :, :, out_lanes]

    def hand_out(pair, i, gone, came):
        src, dst = pair(i)
        to = owner(i)

        @pl.when(to == lon)
        def _():
            pltpu.make_async_copy(src, dst, came.at[group]).start()

        @pl.when(to != lon)
        def _():
            pltpu.make_async_remote_copy(src, dst, gone.at[i], came.at[group], device_id=(lat, to), device_id_type=MESH).start()

    def hand_out_wait(pair, i, gone):
        src, dst = pair(i)
        to = owner(i)

        @pl.when(to != lon)
        def _():
            pltpu.make_async_remote_copy(src, dst, gone.at[i], gone.at[i], device_id=(lat, to), device_id_type=MESH).wait_send()

    own = slice(RADIUS, RADIUS + ROWS)

    def finish_kv(i):
        at = pl.ds(by(SIDE + TILE * tile_of(i, core), SIDE), TILE)
        final_kv[i] = acc[:, own, at].astype(bf16)

    def on_ways(make, then):
        @pl.when(has_above)
        def _():
            then(make(0))

        @pl.when(has_below)
        def _():
            then(make(1))

    def pass_keys(u):
        def go(first):
            size = 3 * TILE if first else STEP
            own_wait(own_kv, u, got_kv, size)
            came_wait(came_kv, u, got_kv, size)
            on_ways(lambda way: relay(u, way, first), lambda copy: copy.start())

        @pl.when(u == 0)
        def _():
            go(True)

        @pl.when(u > 0)
        def _():
            go(False)

    def relay_wait(u, way):
        @pl.when(u == 0)
        def _():
            relay(u, way, True).wait_recv()

        @pl.when(u > 0)
        def _():
            relay(u, way, False).wait_recv()

    last = by((1 - core) * COLS, TILE)

    def compute(i):
        begin = by(tile_of(i, core) * TILE, TILE)
        at, near = pl.ds(begin, TILE), pl.ds(begin, TWIDE)

        def half_tile(half):
            rows = slice(half * HALF, (half + 1) * HALF)
            spans = slice(half * HALF, half * HALF + SPAN)
            q = got_qd[0, rows, at].reshape(HALF * TILE, LANES)
            d = got_qd[1, rows, at].reshape(HALF * TILE, LANES)
            k = got_kv[0, spans, near].reshape(SPAN * TWIDE, LANES)
            v = got_kv[1, spans, near].reshape(SPAN * TWIDE, LANES)
            dq, dk, dv = pair_grads(q, d, k, v, mask[half])
            final_q[i, rows] = dq.astype(bf16).reshape(HALF, TILE, LANES)
            acc[0, spans, near] += dk.reshape(SPAN, TWIDE, LANES)
            acc[1, spans, near] += dv.reshape(SPAN, TWIDE, LANES)

        def send_edge(way):
            rows = (slice(0, RADIUS), slice(TALL - RADIUS, TALL))[way]
            edge_out[i, way] = acc[:, rows, pl.ds(done_at(i), TILE)].astype(bf16)
            edge(i, way).start()

            @pl.when(i == TILES - 1)
            def _():
                last_out[way] = acc[:, rows, pl.ds(last, TILE)].astype(bf16)
                last_edge(way).start()

        @pl.when((i % 2 == 0) & has_above)
        def _():
            relay_wait(i // 2, 1)

        half_tile(0)

        @pl.when(has_above)
        def _():
            send_edge(0)

        @pl.when((i % 2 == 0) & has_below)
        def _():
            relay_wait(i // 2, 0)

        half_tile(1)

        @pl.when(has_below)
        def _():
            send_edge(1)

    def add_edges(i):
        def add(way):
            rows = (slice(ROWS, ROWS + RADIUS), slice(RADIUS, 2 * RADIUS))[way]
            edge(i, way).wait_recv()
            acc[:, rows, pl.ds(done_at(i), TILE)] += edge_in[i, way].astype(f32)

            @pl.when(i == TILES - 1)
            def _():
                last_edge(way).wait_recv()
                acc[:, rows, pl.ds(last, TILE)] += last_in[way].astype(f32)

        @pl.when(has_below)
        def _():
            add(0)

        @pl.when(has_above)
        def _():
            add(1)

        def send_side(n, at):
            cols = pl.ds(by(at, SIDE), SIDE)
            side_out[n] = jnp.concatenate([acc[0, own, cols], acc[1, own, cols]], axis=1).astype(bf16)
            side(n).start()

        @pl.when(i == 0)
        def _():
            send_side(0, core * (WIDE - SIDE))

        @pl.when(i == TILES - 1)
        def _():
            send_side(1, (1 - core) * (WIDE - SIDE))

    def add_side(n, at):
        side(n).wait_recv()
        cols = pl.ds(by(at, SIDE), SIDE)
        got = side_in[n].astype(f32)
        acc[0, own, cols] += got[:, :SIDE]
        acc[1, own, cols] += got[:, SIDE:]

    @pl.loop(0, TILES)
    def _(i):
        @pl.when(i == 0)
        def _():
            pass_keys(0)

        @pl.when(i % 2 == 1)
        def _():
            @pl.when(i < TILES - 1)
            def _():
                pass_keys(i // 2 + 1)

        own_wait(own_qd, i, got_qd, TILE)
        came_wait(came_qd, i, got_qd, TILE)

        compute(i)
        hand_out(q_pair, i, q_gone, q_came)

        @pl.when(i > 0)
        def _():
            add_edges(i - 1)

        @pl.when(i == 2)
        def _():
            add_side(0, either(core, SIDE, COLS))

        @pl.when(i > 1)
        def _():
            finish_kv(i - 2)
            hand_out(kv_pair, i - 2, kv_gone, kv_came)

    add_edges(TILES - 1)
    finish_kv(TILES - 2)
    hand_out(kv_pair, TILES - 2, kv_gone, kv_came)
    add_side(1, either(core, COLS, SIDE))
    finish_kv(TILES - 1)
    hand_out(kv_pair, TILES - 1, kv_gone, kv_came)

    came_wait(sent_kv, 0, got_kv, 3 * TILE)
    on_ways(lambda way: relay(0, way, True), lambda copy: copy.wait_send())

    @pl.loop(1, PARTS)
    def _(u):
        came_wait(sent_kv, u, got_kv, STEP)
        on_ways(lambda way: relay(u, way, False), lambda copy: copy.wait_send())

    on_ways(last_edge, lambda copy: copy.wait_send())
    side(0).wait_send()
    side(1).wait_send()

    @pl.loop(0, TILES)
    def _(i):
        came_wait(sent_qd, i, got_qd, TILE)
        on_ways(lambda way: edge(i, way), lambda copy: copy.wait_send())
        hand_out_wait(q_pair, i, q_gone)
        hand_out_wait(kv_pair, i, kv_gone)
        for pair, came in ((q_pair, q_came), (kv_pair, kv_came)):
            src, dst = pair(i)
            pltpu.make_async_copy(src, dst, came.at[i]).wait()


def on_device(queries, keys, values, grads_out):
    lats = lax.axis_size("lat")
    features = queries.shape[-1]
    vmem = lambda *shape: pltpu.VMEM(shape, bf16)
    sems = lambda *shape: pltpu.SemaphoreType.DMA(shape)
    out = pl.pallas_call(
        functools.partial(kernel, lats),
        out_shape=jax.ShapeDtypeStruct((3, ROWS, TILE, features), bf16),
        in_specs=[pl.BlockSpec(memory_space=pl.ANY)] * 4,
        out_specs=pl.BlockSpec(memory_space=pl.ANY),
        scratch_shapes=[
            vmem(2, LON, features),
            vmem(2, LON + STEP, features),
            vmem(2, LON, features),
            vmem(2, TALL, WIDE, LANES),
            vmem(2, ROWS, COLS, LANES),
            pltpu.VMEM((2, SPAN * TWIDE, 2 * HALF * TILE), f32),
            pltpu.VMEM((2, TALL, WIDE, LANES), f32),
            vmem(TILES, 2, 2, RADIUS, TILE, LANES),
            vmem(TILES, 2, 2, RADIUS, TILE, LANES),
            vmem(2, 2, RADIUS, TILE, LANES),
            vmem(2, 2, RADIUS, TILE, LANES),
            vmem(2, ROWS, 2 * SIDE, LANES),
            vmem(2, ROWS, 2 * SIDE, LANES),
            vmem(TILES, ROWS, TILE, LANES),
            vmem(TILES, 2, ROWS, TILE, LANES),
            sems(4), sems(PARTS), sems(TILES), sems(PARTS), sems(TILES), sems(PARTS), sems(TILES),
            sems(PARTS, 2), sems(PARTS, 2), sems(TILES + 1, 2), sems(TILES + 1, 2), sems(2), sems(2),
            sems(TILES), sems(TILES), sems(TILES), sems(TILES),
        ],
        compiler_params=pltpu.CompilerParams(collective_id=0, has_side_effects=True, vmem_limit_bytes=56 * 1024 * 1024),
    )(queries, keys, values, grads_out)
    return out[0], out[1], out[2]


def solution(mesh):
    placed = P(("lat", "lon"), None, None)
    return jax.shard_map(
        on_device,
        mesh=mesh,
        in_specs=(placed,) * 4,
        out_specs=(P("lat", "lon", None),) * 3,
        check_vma=False,
    )
```

```python
import functools

import jax
import jax.numpy as jnp
from jax import lax
from jax.experimental import pallas as pl
from jax.experimental.pallas import tpu as pltpu
from jax.sharding import PartitionSpec as P

HEAD = 64
LANES = 128
RADIUS = 6
SIDE = 8
LON = 256
ROWS = 16
TILE = 16
TILES = 8
PARTS = 4
STEP = 2 * TILE
COLS = TILES * TILE
WIDE = COLS + 2 * SIDE
TALL = ROWS + 2 * RADIUS
HALF = ROWS // 2
SPAN = HALF + 2 * RADIUS
TWIDE = TILE + 2 * SIDE
DEVICES = 16
OTHERS = DEVICES - 1

MESH = pl.DeviceIdType.MESH
bf16 = jnp.bfloat16
f32 = jnp.float32
masked_score = -1e30


def dot(a, b, ca, cb):
    return lax.dot_general(a, b, (((ca,), (cb,)), ((), ())), preferred_element_type=f32)


def window_mask(lat, lats, half):
    shape = (SPAN * TWIDE, HALF * TILE)
    key = lax.broadcasted_iota(jnp.int32, shape, 0)
    query = lax.broadcasted_iota(jnp.int32, shape, 1)
    down = key // TWIDE - query // TILE
    right = key % TWIDE - query % TILE
    row = lat * ROWS - RADIUS + half * HALF + key // TWIDE
    ok = (down >= 0) & (down <= 2 * RADIUS)
    ok &= (right >= SIDE - RADIUS) & (right <= SIDE + RADIUS)
    ok &= (row >= 0) & (row < lats * ROWS)
    ok = jnp.where(ok, 0.0, masked_score)
    return jnp.concatenate([ok, ok], axis=1)


def pair_grads(q, d, k, v, mask):
    first = lax.broadcasted_iota(jnp.int32, q.shape, 1) < HEAD
    zero = jnp.zeros_like(q)
    q = q * (HEAD ** -0.5)
    q2 = jnp.concatenate([jnp.where(first, q, zero), jnp.where(first, zero, q)], axis=0)
    d2 = jnp.concatenate([jnp.where(first, d, zero), jnp.where(first, zero, d)], axis=0)
    s = dot(k, q2, 1, 1) + mask
    e = jnp.exp(s - jnp.max(s, axis=0, keepdims=True))
    p = e * (1.0 / jnp.sum(e, axis=0, keepdims=True))
    dp = dot(v, d2, 1, 1)
    centre = jnp.sum(p * dp, axis=0, keepdims=True)
    ds = (p * (dp - centre)).astype(bf16)
    dv = dot(p.astype(bf16), d2, 1, 0)
    dk = dot(ds, q2, 1, 0)
    dq = dot(ds, k, 0, 0) * (HEAD ** -0.5)
    count = q.shape[0]
    return jnp.where(first, dq[:count], dq[count:]), dk, dv


HOPS = [(1, 0, 0), (3, 0, 0), (0, 1, 0), (2, 0, 0), (1, 1, 0), (3, 1, 0), (0, 1, 1), (2, 1, 0), (1, 0, 1),
        (3, 0, 1), (2, 0, 1), (1, 1, 1), (3, 1, 1), (2, 1, 1), (0, 0, 1)]


def either(core, a, b):
    return (1 - core) * a + core * b


def by(value, unit):
    return pl.multiple_of(value, unit)


def kernel(lats, q_ref, k_ref, v_ref, d_ref, out_ref, raw, shifted, send_qd, got_kv, got_qd, mask, acc, edge_out, edge_in,
           last_out, last_in, side_out, side_in, final_q, final_kv, load_sem, sent_kv, sent_qd, came_kv, came_qd, own_kv, own_qd,
           relay_out, relay_in, lat_out, lat_in, side_gone, side_came, q_gone, q_came, kv_gone, kv_came):
    lat, lon = lax.axis_index("lat"), lax.axis_index("lon")
    x, z, core = lon // 4, (lon // 2) % 2, lon % 2
    deep = lats // 2
    group = 2 * x + (z + lat // deep) % 2
    partner = (lat, lon + 1 - 2 * core)
    has_above, has_below = lat > 0, lat < lats - 1
    more_above, more_below = (lat + lats - 1) // lats, (2 * lats - 2 - lat) // lats

    def neighbour(other_lat):
        return other_lat, 4 * x + 2 * ((z + lat // deep + other_lat // deep) % 2) + core

    above, below = neighbour(lat - more_above), neighbour(lat + more_below)

    def start_block(g, c):
        return (2 * g + (DEVICES // 2) * c) % DEVICES

    def other(hop):
        ox, oz, oc = (x + hop[0]) % 4, (z + hop[1]) % 2, (core + hop[2]) % 2
        return 4 * ox + 2 * oz + oc, 2 * ox + (oz + lat // deep) % 2, oc

    loads = [pltpu.make_async_copy(r.at[0], t, load_sem.at[i]) for i, (r, t) in enumerate(
        ((k_ref, raw.at[0]), (v_ref, raw.at[1]), (q_ref, send_qd.at[0]), (d_ref, send_qd.at[1])))]
    for load in loads:
        load.start()

    barrier = pltpu.get_barrier_semaphore()
    for hop in HOPS:
        pl.semaphore_signal(barrier, inc=1, device_id=(lat, other(hop)[0]), device_id_type=MESH)

    @pl.when(has_above)
    def _():
        pl.semaphore_signal(barrier, inc=1, device_id=above, device_id_type=MESH)

    @pl.when(has_below)
    def _():
        pl.semaphore_signal(barrier, inc=1, device_id=below, device_id_type=MESH)

    def kv_at(u, c):
        return either(c, 16 + STEP * u, 96 - STEP * u)

    def done_at(i):
        return by(either(core, TILE * i, COLS - TILE * i), TILE)

    def tile_of(i, c):
        return either(c, i, TILES - 1 - i)

    for i in range(2):
        loads[i].wait()
        for g in range(8):
            lanes = slice(g * LANES, (g + 1) * LANES)
            a = raw[i, :, lanes].astype(f32)
            a = jnp.concatenate([a[-SIDE:], a, a[:STEP - SIDE]], axis=0)
            shifted[i, :, lanes] = a.astype(bf16)
    loads[2].wait()
    loads[3].wait()

    pl.semaphore_wait(barrier, OTHERS + more_above + more_below)

    def kv_copy(u, g, c, first):
        off = either(c, 0, 96) if first else kv_at(u, c)
        size = 3 * TILE if first else STEP
        begin = (TILE * start_block(g, c) + off) % LON
        src = shifted.at[:, pl.ds(by(begin, TILE), size), pl.ds(by(g * LANES, LANES), LANES)]
        return src, got_kv.at[:, lon + RADIUS, pl.ds(by(off, TILE), size), :]

    def qd_copy(i, g, c):
        off = TILE * tile_of(i, c)
        begin = (TILE * start_block(g, c) + off) % LON
        src = send_qd.at[:, pl.ds(by(begin, TILE), TILE), pl.ds(by(g * LANES, LANES), LANES)]
        return src, got_qd.at[:, lon, pl.ds(by(off, TILE), TILE), :]

    def spread(pair, i, gone, came, own_sem):
        for hop in HOPS:
            to, g, c = other(hop)
            src, dst = pair(i, g, c)
            pltpu.make_async_remote_copy(src, dst, gone.at[i], came.at[i], device_id=(lat, to), device_id_type=MESH).start()
        src, dst = pair(i, group, core)
        pltpu.make_async_copy(src, dst, own_sem.at[i]).start()

    def spread_kv(u, first=False):
        spread(lambda i, g, c: kv_copy(i, g, c, first), u, sent_kv, came_kv, own_kv)

    def spread_qd(i):
        spread(qd_copy, i, sent_qd, came_qd, own_qd)

    spread_kv(0, True)

    @pl.loop(1, PARTS)
    def _(u):
        spread_kv(u)

        @pl.loop(2 * u - 2, 2 * u)
        def _(i):
            spread_qd(i)

    spread_qd(TILES - 2)
    spread_qd(TILES - 1)

    for half in range(2):
        mask[half] = window_mask(lat, lats, half)

    @pl.loop(0, TALL)
    def _(row):
        acc[:, row] = jnp.zeros((2, WIDE, LANES), f32)

    @pl.when(lat == 0)
    def _():
        got_kv[:, 0:RADIUS] = jnp.zeros((2, RADIUS, WIDE, LANES), bf16)

    @pl.when(lat == lats - 1)
    def _():
        got_kv[:, TALL - RADIUS:TALL] = jnp.zeros((2, RADIUS, WIDE, LANES), bf16)

    def came_wait(sem, u, ref, size):
        blank = ref.at[:, 0:OTHERS, 0:size, :]
        pltpu.make_async_copy(blank, blank, sem.at[u]).wait()

    def own_wait(sem, u, ref, size):
        blank = ref.at[:, 0, 0:size, :]
        pltpu.make_async_copy(blank, blank, sem.at[u]).wait()

    def relay(u, way, first):
        off = either(core, 0, 96) if first else kv_at(u, core)
        cols = pl.ds(by(off, TILE), 3 * TILE if first else STEP)
        here, there, to = ((slice(RADIUS, 2 * RADIUS), slice(TALL - RADIUS, TALL), above),
                           (slice(ROWS, ROWS + RADIUS), slice(0, RADIUS), below))[way]
        return pltpu.make_async_remote_copy(got_kv.at[:, here, cols, :], got_kv.at[:, there, cols, :], relay_out.at[u, way],
                                            relay_in.at[u, way], device_id=to, device_id_type=MESH)

    def edge(u, way):
        return pltpu.make_async_remote_copy(edge_out.at[u, way], edge_in.at[u, way], lat_out.at[u, way], lat_in.at[u, way],
                                            device_id=(above, below)[way], device_id_type=MESH)

    def last_edge(way):
        return pltpu.make_async_remote_copy(last_out.at[way], last_in.at[way], lat_out.at[TILES, way], lat_in.at[TILES, way],
                                            device_id=(above, below)[way], device_id_type=MESH)

    def side(i):
        return pltpu.make_async_remote_copy(side_out.at[i], side_in.at[i], side_gone.at[i], side_came.at[i],
                                            device_id=partner, device_id_type=MESH)

    out_lanes = pl.ds(by(group * LANES, LANES), LANES)

    def owner(i):
        return (start_block(group, core) + tile_of(i, core)) % DEVICES

    def q_pair(i):
        return final_q.at[i], out_ref.at[0, :, :, out_lanes]

    def kv_pair(i):
        return final_kv.at[i], out_ref.at[1:3, :, :, out_lanes]

    def hand_out(pair, i, gone, came):
        src, dst = pair(i)
        to = owner(i)

        @pl.when(to == lon)
        def _():
            pltpu.make_async_copy(src, dst, came.at[group]).start()

        @pl.when(to != lon)
        def _():
            pltpu.make_async_remote_copy(src, dst, gone.at[i], came.at[group], device_id=(lat, to), device_id_type=MESH).start()

    def hand_out_wait(pair, i, gone):
        src, dst = pair(i)
        to = owner(i)

        @pl.when(to != lon)
        def _():
            pltpu.make_async_remote_copy(src, dst, gone.at[i], gone.at[i], device_id=(lat, to), device_id_type=MESH).wait_send()

    own = slice(RADIUS, RADIUS + ROWS)

    def finish_kv(i):
        at = pl.ds(by(SIDE + TILE * tile_of(i, core), SIDE), TILE)
        final_kv[i] = acc[:, own, at].astype(bf16)

    def on_ways(make, then):
        @pl.when(has_above)
        def _():
            then(make(0))

        @pl.when(has_below)
        def _():
            then(make(1))

    def pass_keys(u):
        def go(first):
            size = 3 * TILE if first else STEP
            own_wait(own_kv, u, got_kv, size)
            came_wait(came_kv, u, got_kv, size)
            on_ways(lambda way: relay(u, way, first), lambda copy: copy.start())

        @pl.when(u == 0)
        def _():
            go(True)

        @pl.when(u > 0)
        def _():
            go(False)

    def relay_wait(u, way):
        @pl.when(u == 0)
        def _():
            relay(u, way, True).wait_recv()

        @pl.when(u > 0)
        def _():
            relay(u, way, False).wait_recv()

    last = by((1 - core) * COLS, TILE)

    def compute(i):
        begin = by(tile_of(i, core) * TILE, TILE)
        at, near = pl.ds(begin, TILE), pl.ds(begin, TWIDE)

        def half_tile(half):
            rows = slice(half * HALF, (half + 1) * HALF)
            spans = slice(half * HALF, half * HALF + SPAN)
            q = got_qd[0, rows, at].reshape(HALF * TILE, LANES)
            d = got_qd[1, rows, at].reshape(HALF * TILE, LANES)
            k = got_kv[0, spans, near].reshape(SPAN * TWIDE, LANES)
            v = got_kv[1, spans, near].reshape(SPAN * TWIDE, LANES)
            dq, dk, dv = pair_grads(q, d, k, v, mask[half])
            final_q[i, rows] = dq.astype(bf16).reshape(HALF, TILE, LANES)
            acc[0, spans, near] += dk.reshape(SPAN, TWIDE, LANES)
            acc[1, spans, near] += dv.reshape(SPAN, TWIDE, LANES)

        def send_edge(way):
            rows = (slice(0, RADIUS), slice(TALL - RADIUS, TALL))[way]
            edge_out[i, way] = acc[:, rows, pl.ds(done_at(i), TILE)].astype(bf16)
            edge(i, way).start()

            @pl.when(i == TILES - 1)
            def _():
                last_out[way] = acc[:, rows, pl.ds(last, TILE)].astype(bf16)
                last_edge(way).start()

        @pl.when((i % 2 == 0) & has_above)
        def _():
            relay_wait(i // 2, 1)

        half_tile(0)

        @pl.when(has_above)
        def _():
            send_edge(0)

        @pl.when((i % 2 == 0) & has_below)
        def _():
            relay_wait(i // 2, 0)

        half_tile(1)

        @pl.when(has_below)
        def _():
            send_edge(1)

    def add_edges(i):
        def add(way):
            rows = (slice(ROWS, ROWS + RADIUS), slice(RADIUS, 2 * RADIUS))[way]
            edge(i, way).wait_recv()
            acc[:, rows, pl.ds(done_at(i), TILE)] += edge_in[i, way].astype(f32)

            @pl.when(i == TILES - 1)
            def _():
                last_edge(way).wait_recv()
                acc[:, rows, pl.ds(last, TILE)] += last_in[way].astype(f32)

        @pl.when(has_below)
        def _():
            add(0)

        @pl.when(has_above)
        def _():
            add(1)

        def send_side(n, at):
            cols = pl.ds(by(at, SIDE), SIDE)
            side_out[n] = jnp.concatenate([acc[0, own, cols], acc[1, own, cols]], axis=1).astype(bf16)
            side(n).start()

        @pl.when(i == 0)
        def _():
            send_side(0, core * (WIDE - SIDE))

        @pl.when(i == TILES - 1)
        def _():
            send_side(1, (1 - core) * (WIDE - SIDE))

    def add_side(n, at):
        side(n).wait_recv()
        cols = pl.ds(by(at, SIDE), SIDE)
        got = side_in[n].astype(f32)
        acc[0, own, cols] += got[:, :SIDE]
        acc[1, own, cols] += got[:, SIDE:]

    @pl.loop(0, TILES)
    def _(i):
        @pl.when(i == 0)
        def _():
            pass_keys(0)

        @pl.when((i % 2 == 0) & (i < TILES - 2))
        def _():
            pass_keys(i // 2 + 1)

        own_wait(own_qd, i, got_qd, TILE)
        came_wait(came_qd, i, got_qd, TILE)

        compute(i)
        hand_out(q_pair, i, q_gone, q_came)

        @pl.when(i > 1)
        def _():
            add_edges(i - 2)

        @pl.when(i == 3)
        def _():
            add_side(0, either(core, SIDE, COLS))

        @pl.when(i > 2)
        def _():
            finish_kv(i - 3)
            hand_out(kv_pair, i - 3, kv_gone, kv_came)

    add_edges(TILES - 2)
    finish_kv(TILES - 3)
    hand_out(kv_pair, TILES - 3, kv_gone, kv_came)
    add_edges(TILES - 1)
    finish_kv(TILES - 2)
    hand_out(kv_pair, TILES - 2, kv_gone, kv_came)
    add_side(1, either(core, COLS, SIDE))
    finish_kv(TILES - 1)
    hand_out(kv_pair, TILES - 1, kv_gone, kv_came)

    came_wait(sent_kv, 0, got_kv, 3 * TILE)
    on_ways(lambda way: relay(0, way, True), lambda copy: copy.wait_send())

    @pl.loop(1, PARTS)
    def _(u):
        came_wait(sent_kv, u, got_kv, STEP)
        on_ways(lambda way: relay(u, way, False), lambda copy: copy.wait_send())

    on_ways(last_edge, lambda copy: copy.wait_send())
    side(0).wait_send()
    side(1).wait_send()

    @pl.loop(0, TILES)
    def _(i):
        came_wait(sent_qd, i, got_qd, TILE)
        on_ways(lambda way: edge(i, way), lambda copy: copy.wait_send())
        hand_out_wait(q_pair, i, q_gone)
        hand_out_wait(kv_pair, i, kv_gone)
        for pair, came in ((q_pair, q_came), (kv_pair, kv_came)):
            src, dst = pair(i)
            pltpu.make_async_copy(src, dst, came.at[i]).wait()


def on_device(queries, keys, values, grads_out):
    lats = lax.axis_size("lat")
    features = queries.shape[-1]
    vmem = lambda *shape: pltpu.VMEM(shape, bf16)
    sems = lambda *shape: pltpu.SemaphoreType.DMA(shape)
    out = pl.pallas_call(
        functools.partial(kernel, lats),
        out_shape=jax.ShapeDtypeStruct((3, ROWS, TILE, features), bf16),
        in_specs=[pl.BlockSpec(memory_space=pl.ANY)] * 4,
        out_specs=pl.BlockSpec(memory_space=pl.ANY),
        scratch_shapes=[
            vmem(2, LON, features),
            vmem(2, LON + STEP, features),
            vmem(2, LON, features),
            vmem(2, TALL, WIDE, LANES),
            vmem(2, ROWS, COLS, LANES),
            pltpu.VMEM((2, SPAN * TWIDE, 2 * HALF * TILE), f32),
            pltpu.VMEM((2, TALL, WIDE, LANES), f32),
            vmem(TILES, 2, 2, RADIUS, TILE, LANES),
            vmem(TILES, 2, 2, RADIUS, TILE, LANES),
            vmem(2, 2, RADIUS, TILE, LANES),
            vmem(2, 2, RADIUS, TILE, LANES),
            vmem(2, ROWS, 2 * SIDE, LANES),
            vmem(2, ROWS, 2 * SIDE, LANES),
            vmem(TILES, ROWS, TILE, LANES),
            vmem(TILES, 2, ROWS, TILE, LANES),
            sems(4), sems(PARTS), sems(TILES), sems(PARTS), sems(TILES), sems(PARTS), sems(TILES),
            sems(PARTS, 2), sems(PARTS, 2), sems(TILES + 1, 2), sems(TILES + 1, 2), sems(2), sems(2),
            sems(TILES), sems(TILES), sems(TILES), sems(TILES),
        ],
        compiler_params=pltpu.CompilerParams(collective_id=0, has_side_effects=True, vmem_limit_bytes=56 * 1024 * 1024),
    )(queries, keys, values, grads_out)
    return out[0], out[1], out[2]


def solution(mesh):
    placed = P(("lat", "lon"), None, None)
    return jax.shard_map(
        on_device,
        mesh=mesh,
        in_specs=(placed,) * 4,
        out_specs=(P("lat", "lon", None),) * 3,
        check_vma=False,
    )
```

```python
import functools

import jax
import jax.numpy as jnp
from jax import lax
from jax.experimental import pallas as pl
from jax.experimental.pallas import tpu as pltpu
from jax.sharding import PartitionSpec as P

HEAD = 64
LANES = 128
RADIUS = 6
SIDE = 8
LON = 256
ROWS = 16
TILE = 16
TILES = 8
PIECES = 4
PARTS = 4
STEP = 2 * TILE
COLS = TILES * TILE
WIDE = COLS + 2 * SIDE
TALL = ROWS + 2 * RADIUS
HALF = ROWS // 2
SPAN = HALF + 2 * RADIUS
TWIDE = TILE + 2 * SIDE
DEVICES = 16
OTHERS = DEVICES - 1

MESH = pl.DeviceIdType.MESH
bf16 = jnp.bfloat16
f32 = jnp.float32
masked_score = -1e30


def dot(a, b, ca, cb):
    return lax.dot_general(a, b, (((ca,), (cb,)), ((), ())), preferred_element_type=f32)


def window_mask(lat, lats, half):
    shape = (SPAN * TWIDE, HALF * TILE)
    key = lax.broadcasted_iota(jnp.int32, shape, 0)
    query = lax.broadcasted_iota(jnp.int32, shape, 1)
    down = key // TWIDE - query // TILE
    right = key % TWIDE - query % TILE
    row = lat * ROWS - RADIUS + half * HALF + key // TWIDE
    ok = (down >= 0) & (down <= 2 * RADIUS)
    ok &= (right >= SIDE - RADIUS) & (right <= SIDE + RADIUS)
    ok &= (row >= 0) & (row < lats * ROWS)
    ok = jnp.where(ok, 0.0, masked_score)
    return jnp.concatenate([ok, ok], axis=1)


def pair_grads(q, d, k, v, mask):
    first = lax.broadcasted_iota(jnp.int32, q.shape, 1) < HEAD
    zero = jnp.zeros_like(q)
    q = q * (HEAD ** -0.5)
    q2 = jnp.concatenate([jnp.where(first, q, zero), jnp.where(first, zero, q)], axis=0)
    d2 = jnp.concatenate([jnp.where(first, d, zero), jnp.where(first, zero, d)], axis=0)
    s = dot(k, q2, 1, 1) + mask
    e = jnp.exp(s - jnp.max(s, axis=0, keepdims=True))
    p = e * (1.0 / jnp.sum(e, axis=0, keepdims=True))
    dp = dot(v, d2, 1, 1)
    centre = jnp.sum(p * dp, axis=0, keepdims=True)
    ds = (p * (dp - centre)).astype(bf16)
    dv = dot(p.astype(bf16), d2, 1, 0)
    dk = dot(ds, q2, 1, 0)
    dq = dot(ds, k, 0, 0) * (HEAD ** -0.5)
    count = q.shape[0]
    return jnp.where(first, dq[:count], dq[count:]), dk, dv


HOPS = [(1, 0, 0), (3, 0, 0), (0, 1, 0), (2, 0, 0), (1, 1, 0), (3, 1, 0), (0, 1, 1), (2, 1, 0), (1, 0, 1),
        (3, 0, 1), (2, 0, 1), (1, 1, 1), (3, 1, 1), (2, 1, 1), (0, 0, 1)]


def either(core, a, b):
    return (1 - core) * a + core * b


def by(value, unit):
    return pl.multiple_of(value, unit)


def kernel(lats, q_ref, k_ref, v_ref, d_ref, out_ref, raw, shifted, send_qd, got_kv, got_qd, mask, acc, edge_out, edge_in,
           last_out, last_in, side_out, side_in, final_q, final_kv, load_sem, sent_kv, sent_qd, came_kv, came_qd, own_kv, own_qd,
           relay_out, relay_in, lat_out, lat_in, side_gone, side_came, q_gone, q_came, kv_gone, kv_came):
    lat, lon = lax.axis_index("lat"), lax.axis_index("lon")
    x, z, core = lon // 4, (lon // 2) % 2, lon % 2
    deep = lats // 2
    group = 2 * x + (z + lat // deep) % 2
    partner = (lat, lon + 1 - 2 * core)
    has_above, has_below = lat > 0, lat < lats - 1
    more_above, more_below = (lat + lats - 1) // lats, (2 * lats - 2 - lat) // lats

    def neighbour(other_lat):
        return other_lat, 4 * x + 2 * ((z + lat // deep + other_lat // deep) % 2) + core

    above, below = neighbour(lat - more_above), neighbour(lat + more_below)

    def start_block(g, c):
        return (2 * g + 10 + (DEVICES // 2) * c) % DEVICES

    def other(hop):
        ox, oz, oc = (x + hop[0]) % 4, (z + hop[1]) % 2, (core + hop[2]) % 2
        return 4 * ox + 2 * oz + oc, 2 * ox + (oz + lat // deep) % 2, oc

    loads = [pltpu.make_async_copy(r.at[0], t, load_sem.at[i]) for i, (r, t) in enumerate(
        ((k_ref, raw.at[0]), (v_ref, raw.at[1]), (q_ref, send_qd.at[0]), (d_ref, send_qd.at[1])))]

    barrier = pltpu.get_barrier_semaphore()
    for hop in HOPS:
        pl.semaphore_signal(barrier, inc=1, device_id=(lat, other(hop)[0]), device_id_type=MESH)

    @pl.when(has_above)
    def _():
        pl.semaphore_signal(barrier, inc=1, device_id=above, device_id_type=MESH)

    @pl.when(has_below)
    def _():
        pl.semaphore_signal(barrier, inc=1, device_id=below, device_id_type=MESH)

    for load in loads:
        load.start()

    def kv_at(u, c):
        return either(c, 16 + STEP * u, 96 - STEP * u)

    def done_at(i):
        return by(either(core, TILE * i, COLS - TILE * i), TILE)

    def tile_of(i, c):
        return either(c, i, TILES - 1 - i)

    for i in range(2):
        loads[i].wait()
        for g in range(8):
            lanes = slice(g * LANES, (g + 1) * LANES)
            a = raw[i, :, lanes].astype(f32)
            a = jnp.concatenate([a[-SIDE:], a, a[:STEP - SIDE]], axis=0)
            shifted[i, :, lanes] = a.astype(bf16)
    loads[2].wait()
    loads[3].wait()

    pl.semaphore_wait(barrier, OTHERS + more_above + more_below)

    def kv_copy(u, g, c, first):
        off = either(c, 0, 96) if first else kv_at(u, c)
        size = 3 * TILE if first else STEP
        begin = (TILE * start_block(g, c) + off) % LON
        src = shifted.at[:, pl.ds(by(begin, TILE), size), pl.ds(by(g * LANES, LANES), LANES)]
        return src, got_kv.at[:, lon + RADIUS, pl.ds(by(off, TILE), size), :]

    def qd_copy(i, g, c):
        off = TILE * tile_of(i, c)
        begin = (TILE * start_block(g, c) + off) % LON
        src = send_qd.at[:, pl.ds(by(begin, TILE), TILE), pl.ds(by(g * LANES, LANES), LANES)]
        return src, got_qd.at[:, lon, pl.ds(by(off, TILE), TILE), :]

    def spread(pair, i, gone, came, own_sem):
        for hop in HOPS:
            to, g, c = other(hop)
            src, dst = pair(i, g, c)
            pltpu.make_async_remote_copy(src, dst, gone.at[i], came.at[i], device_id=(lat, to), device_id_type=MESH).start()
        src, dst = pair(i, group, core)
        pltpu.make_async_copy(src, dst, own_sem.at[i]).start()

    def spread_kv(u, first=False):
        spread(lambda i, g, c: kv_copy(i, g, c, first), u, sent_kv, came_kv, own_kv)

    def spread_qd(i):
        spread(qd_copy, i, sent_qd, came_qd, own_qd)

    spread_kv(0, True)

    @pl.loop(1, PARTS)
    def _(u):
        spread_kv(u)

        @pl.loop(2 * u - 2, 2 * u)
        def _(i):
            spread_qd(i)

    spread_qd(TILES - 2)
    spread_qd(TILES - 1)

    for half in range(2):
        mask[half] = window_mask(lat, lats, half)

    @pl.loop(0, TALL)
    def _(row):
        acc[:, row] = jnp.zeros((2, WIDE, LANES), f32)

    @pl.when(lat == 0)
    def _():
        got_kv[:, 0:RADIUS] = jnp.zeros((2, RADIUS, WIDE, LANES), bf16)

    @pl.when(lat == lats - 1)
    def _():
        got_kv[:, TALL - RADIUS:TALL] = jnp.zeros((2, RADIUS, WIDE, LANES), bf16)

    def came_wait(sem, u, ref, size):
        blank = ref.at[:, 0:OTHERS, 0:size, :]
        pltpu.make_async_copy(blank, blank, sem.at[u]).wait()

    def own_wait(sem, u, ref, size):
        blank = ref.at[:, 0, 0:size, :]
        pltpu.make_async_copy(blank, blank, sem.at[u]).wait()

    def relay(u, way, first):
        off = either(core, 0, 96) if first else kv_at(u, core)
        cols = pl.ds(by(off, TILE), 3 * TILE if first else STEP)
        here, there, to = ((slice(RADIUS, 2 * RADIUS), slice(TALL - RADIUS, TALL), above),
                           (slice(ROWS, ROWS + RADIUS), slice(0, RADIUS), below))[way]
        return pltpu.make_async_remote_copy(got_kv.at[:, here, cols, :], got_kv.at[:, there, cols, :], relay_out.at[u, way],
                                            relay_in.at[u, way], device_id=to, device_id_type=MESH)

    def edge(u, way):
        return pltpu.make_async_remote_copy(edge_out.at[u, way], edge_in.at[u, way], lat_out.at[u, way], lat_in.at[u, way],
                                            device_id=(above, below)[way], device_id_type=MESH)

    def last_edge(way):
        return pltpu.make_async_remote_copy(last_out.at[way], last_in.at[way], lat_out.at[TILES, way], lat_in.at[TILES, way],
                                            device_id=(above, below)[way], device_id_type=MESH)

    def side(i):
        return pltpu.make_async_remote_copy(side_out.at[i], side_in.at[i], side_gone.at[i], side_came.at[i],
                                            device_id=partner, device_id_type=MESH)

    out_lanes = pl.ds(by(group * LANES, LANES), LANES)

    def owner(i):
        return (start_block(group, core) + tile_of(i, core)) % DEVICES

    def q_pair(i):
        return final_q.at[i], out_ref.at[0, :, :, out_lanes]

    def kv_pair(i):
        return final_kv.at[i], out_ref.at[1:3, :, :, out_lanes]

    def hand_out(pair, i, gone, came):
        src, dst = pair(i)
        to = owner(i)

        @pl.when(to == lon)
        def _():
            pltpu.make_async_copy(src, dst, came.at[group]).start()

        @pl.when(to != lon)
        def _():
            pltpu.make_async_remote_copy(src, dst, gone.at[i], came.at[group], device_id=(lat, to), device_id_type=MESH).start()

    def hand_out_wait(pair, i, gone):
        src, dst = pair(i)
        to = owner(i)

        @pl.when(to != lon)
        def _():
            pltpu.make_async_remote_copy(src, dst, gone.at[i], gone.at[i], device_id=(lat, to), device_id_type=MESH).wait_send()

    own = slice(RADIUS, RADIUS + ROWS)

    def finish_kv(i):
        at = pl.ds(by(SIDE + TILE * tile_of(i, core), SIDE), TILE)
        final_kv[i] = acc[:, own, at].astype(bf16)

    def on_ways(make, then):
        @pl.when(has_above)
        def _():
            then(make(0))

        @pl.when(has_below)
        def _():
            then(make(1))

    def pass_keys(u):
        def go(first):
            size = 3 * TILE if first else STEP
            own_wait(own_kv, u, got_kv, size)
            came_wait(came_kv, u, got_kv, size)
            on_ways(lambda way: relay(u, way, first), lambda copy: copy.start())

        @pl.when(u == 0)
        def _():
            go(True)

        @pl.when(u > 0)
        def _():
            go(False)

    def relay_wait(u, way):
        @pl.when(u == 0)
        def _():
            relay(u, way, True).wait_recv()

        @pl.when(u > 0)
        def _():
            relay(u, way, False).wait_recv()

    last = by((1 - core) * COLS, TILE)

    def compute(i):
        begin = by(tile_of(i, core) * TILE, TILE)
        at, near = pl.ds(begin, TILE), pl.ds(begin, TWIDE)

        def half_tile(half):
            rows = slice(half * HALF, (half + 1) * HALF)
            spans = slice(half * HALF, half * HALF + SPAN)
            q = got_qd[0, rows, at].reshape(HALF * TILE, LANES)
            d = got_qd[1, rows, at].reshape(HALF * TILE, LANES)
            k = got_kv[0, spans, near].reshape(SPAN * TWIDE, LANES)
            v = got_kv[1, spans, near].reshape(SPAN * TWIDE, LANES)
            dq, dk, dv = pair_grads(q, d, k, v, mask[half])
            final_q[i, rows] = dq.astype(bf16).reshape(HALF, TILE, LANES)
            acc[0, spans, near] += dk.reshape(SPAN, TWIDE, LANES)
            acc[1, spans, near] += dv.reshape(SPAN, TWIDE, LANES)

        def send_edge(way):
            rows = (slice(0, RADIUS), slice(TALL - RADIUS, TALL))[way]
            edge_out[i, way] = acc[:, rows, pl.ds(done_at(i), TILE)].astype(bf16)
            edge(i, way).start()

            @pl.when(i == TILES - 1)
            def _():
                last_out[way] = acc[:, rows, pl.ds(last, TILE)].astype(bf16)
                last_edge(way).start()

        @pl.when((i % 2 == 0) & has_above)
        def _():
            relay_wait(i // 2, 1)

        half_tile(0)

        @pl.when(has_above)
        def _():
            send_edge(0)

        @pl.when((i % 2 == 0) & has_below)
        def _():
            relay_wait(i // 2, 0)

        half_tile(1)

        @pl.when(has_below)
        def _():
            send_edge(1)

    def add_edges(i):
        def add(way):
            rows = (slice(ROWS, ROWS + RADIUS), slice(RADIUS, 2 * RADIUS))[way]
            edge(i, way).wait_recv()
            acc[:, rows, pl.ds(done_at(i), TILE)] += edge_in[i, way].astype(f32)

            @pl.when(i == TILES - 1)
            def _():
                last_edge(way).wait_recv()
                acc[:, rows, pl.ds(last, TILE)] += last_in[way].astype(f32)

        @pl.when(has_below)
        def _():
            add(0)

        @pl.when(has_above)
        def _():
            add(1)

        def send_side(n, at):
            cols = pl.ds(by(at, SIDE), SIDE)
            side_out[n] = jnp.concatenate([acc[0, own, cols], acc[1, own, cols]], axis=1).astype(bf16)
            side(n).start()

        @pl.when(i == 0)
        def _():
            send_side(0, core * (WIDE - SIDE))

        @pl.when(i == TILES - 1)
        def _():
            send_side(1, (1 - core) * (WIDE - SIDE))

    def add_side(n, at):
        side(n).wait_recv()
        cols = pl.ds(by(at, SIDE), SIDE)
        got = side_in[n].astype(f32)
        acc[0, own, cols] += got[:, :SIDE]
        acc[1, own, cols] += got[:, SIDE:]

    @pl.loop(0, TILES)
    def _(i):
        @pl.when(i == 0)
        def _():
            pass_keys(0)

        @pl.when((i % 2 == 0) & (i < TILES - 2))
        def _():
            pass_keys(i // 2 + 1)

        own_wait(own_qd, i, got_qd, TILE)
        came_wait(came_qd, i, got_qd, TILE)

        compute(i)
        hand_out(q_pair, i, q_gone, q_came)

        @pl.when(i > 1)
        def _():
            add_edges(i - 2)

        @pl.when(i == 3)
        def _():
            add_side(0, either(core, SIDE, COLS))

        @pl.when(i > 2)
        def _():
            finish_kv(i - 3)
            hand_out(kv_pair, i - 3, kv_gone, kv_came)

    add_edges(TILES - 2)
    finish_kv(TILES - 3)
    hand_out(kv_pair, TILES - 3, kv_gone, kv_came)
    add_edges(TILES - 1)
    finish_kv(TILES - 2)
    hand_out(kv_pair, TILES - 2, kv_gone, kv_came)
    add_side(1, either(core, COLS, SIDE))
    finish_kv(TILES - 1)
    hand_out(kv_pair, TILES - 1, kv_gone, kv_came)

    came_wait(sent_kv, 0, got_kv, 3 * TILE)
    on_ways(lambda way: relay(0, way, True), lambda copy: copy.wait_send())

    @pl.loop(1, PARTS)
    def _(u):
        came_wait(sent_kv, u, got_kv, STEP)
        on_ways(lambda way: relay(u, way, False), lambda copy: copy.wait_send())

    on_ways(last_edge, lambda copy: copy.wait_send())
    side(0).wait_send()
    side(1).wait_send()

    @pl.loop(0, TILES)
    def _(i):
        came_wait(sent_qd, i, got_qd, TILE)
        on_ways(lambda way: edge(i, way), lambda copy: copy.wait_send())
        hand_out_wait(q_pair, i, q_gone)
        hand_out_wait(kv_pair, i, kv_gone)
        for pair, came in ((q_pair, q_came), (kv_pair, kv_came)):
            src, dst = pair(i)
            pltpu.make_async_copy(src, dst, came.at[i]).wait()


def part_kernel(all_ref, *refs):
    outs, (held, load_sem, store_sem) = refs[:3], refs[3:]
    size = ROWS // PIECES
    pairs = [(i, j, slice(j * size, (j + 1) * size)) for i in range(3) for j in range(PIECES)]
    loads = [pltpu.make_async_copy(all_ref.at[i, s], held.at[i, s], load_sem.at[i, j]) for i, j, s in pairs]
    stores = [pltpu.make_async_copy(held.at[i, s], outs[i].at[s], store_sem.at[i, j]) for i, j, s in pairs]
    for load in loads:
        load.start()
    for load, store in zip(loads, stores):
        load.wait()
        store.start()
    for store in stores:
        store.wait()


def on_device(queries, keys, values, grads_out):
    lats = lax.axis_size("lat")
    features = queries.shape[-1]
    vmem = lambda *shape: pltpu.VMEM(shape, bf16)
    sems = lambda *shape: pltpu.SemaphoreType.DMA(shape)
    out = pl.pallas_call(
        functools.partial(kernel, lats),
        out_shape=jax.ShapeDtypeStruct((3, ROWS, TILE, features), bf16),
        in_specs=[pl.BlockSpec(memory_space=pl.ANY)] * 4,
        out_specs=pl.BlockSpec(memory_space=pl.ANY),
        scratch_shapes=[
            vmem(2, LON, features),
            vmem(2, LON + STEP, features),
            vmem(2, LON, features),
            vmem(2, TALL, WIDE, LANES),
            vmem(2, ROWS, COLS, LANES),
            pltpu.VMEM((2, SPAN * TWIDE, 2 * HALF * TILE), f32),
            pltpu.VMEM((2, TALL, WIDE, LANES), f32),
            vmem(TILES, 2, 2, RADIUS, TILE, LANES),
            vmem(TILES, 2, 2, RADIUS, TILE, LANES),
            vmem(2, 2, RADIUS, TILE, LANES),
            vmem(2, 2, RADIUS, TILE, LANES),
            vmem(2, ROWS, 2 * SIDE, LANES),
            vmem(2, ROWS, 2 * SIDE, LANES),
            vmem(TILES, ROWS, TILE, LANES),
            vmem(TILES, 2, ROWS, TILE, LANES),
            sems(4), sems(PARTS), sems(TILES), sems(PARTS), sems(TILES), sems(PARTS), sems(TILES),
            sems(PARTS, 2), sems(PARTS, 2), sems(TILES + 1, 2), sems(TILES + 1, 2), sems(2), sems(2),
            sems(TILES), sems(TILES), sems(TILES), sems(TILES),
        ],
        compiler_params=pltpu.CompilerParams(collective_id=0, has_side_effects=True, vmem_limit_bytes=56 * 1024 * 1024),
    )(queries, keys, values, grads_out)
    shape = jax.ShapeDtypeStruct(out.shape[1:], bf16)
    return pl.pallas_call(
        part_kernel,
        in_specs=[pl.BlockSpec(memory_space=pl.ANY)],
        out_specs=[pl.BlockSpec(memory_space=pl.ANY)] * 3,
        out_shape=[shape] * 3,
        scratch_shapes=[pltpu.VMEM(out.shape, bf16), sems(3, PIECES), sems(3, PIECES)],
    )(out)


def solution(mesh):
    placed = P(("lat", "lon"), None, None)
    return jax.shard_map(
        on_device,
        mesh=mesh,
        in_specs=(placed,) * 4,
        out_specs=(P("lat", "lon", None),) * 3,
        check_vma=False,
    )
```

```python
import functools

import jax
import jax.numpy as jnp
from jax import lax
from jax.experimental import pallas as pl
from jax.experimental.pallas import tpu as pltpu
from jax.sharding import PartitionSpec as P

HEAD = 64
LANES = 128
RADIUS = 6
SIDE = 8
LON = 256
ROWS = 16
TILE = 16
TILES = 8
PIECES = 4
PARTS = 4
STEP = 2 * TILE
COLS = TILES * TILE
WIDE = COLS + 2 * SIDE
TALL = ROWS + 2 * RADIUS
HALF = ROWS // 2
SPAN = HALF + 2 * RADIUS
TWIDE = TILE + 2 * SIDE
DEVICES = 16
OTHERS = DEVICES - 1

MESH = pl.DeviceIdType.MESH
bf16 = jnp.bfloat16
f32 = jnp.float32
masked_score = -1e30


def dot(a, b, ca, cb):
    return lax.dot_general(a, b, (((ca,), (cb,)), ((), ())), preferred_element_type=f32)


def window_mask(lat, lats, half):
    shape = (SPAN * TWIDE, HALF * TILE)
    key = lax.broadcasted_iota(jnp.int32, shape, 0)
    query = lax.broadcasted_iota(jnp.int32, shape, 1)
    down = key // TWIDE - query // TILE
    right = key % TWIDE - query % TILE
    row = lat * ROWS - RADIUS + half * HALF + key // TWIDE
    ok = (down >= 0) & (down <= 2 * RADIUS)
    ok &= (right >= SIDE - RADIUS) & (right <= SIDE + RADIUS)
    ok &= (row >= 0) & (row < lats * ROWS)
    ok = jnp.where(ok, 0.0, masked_score)
    return jnp.concatenate([ok, ok], axis=1)


def pair_grads(q, d, k, v, mask):
    first = lax.broadcasted_iota(jnp.int32, q.shape, 1) < HEAD
    zero = jnp.zeros_like(q)
    q = q * (HEAD ** -0.5)
    q2 = jnp.concatenate([jnp.where(first, q, zero), jnp.where(first, zero, q)], axis=0)
    d2 = jnp.concatenate([jnp.where(first, d, zero), jnp.where(first, zero, d)], axis=0)
    s = dot(k, q2, 1, 1) + mask
    e = jnp.exp(s - jnp.max(s, axis=0, keepdims=True))
    p = e * (1.0 / jnp.sum(e, axis=0, keepdims=True))
    dp = dot(v, d2, 1, 1)
    centre = jnp.sum(p * dp, axis=0, keepdims=True)
    ds = (p * (dp - centre)).astype(bf16)
    dv = dot(p.astype(bf16), d2, 1, 0)
    dk = dot(ds, q2, 1, 0)
    dq = dot(ds, k, 0, 0) * (HEAD ** -0.5)
    count = q.shape[0]
    return jnp.where(first, dq[:count], dq[count:]), dk, dv


HOPS = [(2, 1, 0), (1, 0, 0), (3, 0, 1), (2, 0, 1), (0, 1, 0), (1, 1, 1), (3, 1, 0), (2, 0, 0), (2, 1, 1),
        (1, 0, 1), (3, 0, 0), (0, 1, 1), (1, 1, 0), (3, 1, 1), (0, 0, 1)]


def either(core, a, b):
    return (1 - core) * a + core * b


def by(value, unit):
    return pl.multiple_of(value, unit)


def kernel(lats, q_ref, k_ref, v_ref, d_ref, out_ref, raw, shifted, send_qd, got_kv, got_qd, mask, acc, edge_out, edge_in,
           last_out, last_in, side_out, side_in, final_q, final_kv, load_sem, sent_kv, sent_qd, came_kv, came_qd, own_kv, own_qd,
           relay_out, relay_in, lat_out, lat_in, side_gone, side_came, q_gone, q_came, kv_gone, kv_came):
    lat, lon = lax.axis_index("lat"), lax.axis_index("lon")
    x, z, core = lon // 4, (lon // 2) % 2, lon % 2
    deep = lats // 2
    group = 2 * x + (z + lat // deep) % 2
    partner = (lat, lon + 1 - 2 * core)
    has_above, has_below = lat > 0, lat < lats - 1
    more_above, more_below = (lat + lats - 1) // lats, (2 * lats - 2 - lat) // lats

    def neighbour(other_lat):
        return other_lat, 4 * x + 2 * ((z + lat // deep + other_lat // deep) % 2) + core

    above, below = neighbour(lat - more_above), neighbour(lat + more_below)

    def start_block(g, c):
        return (2 * g + 10 + (DEVICES // 2) * c) % DEVICES

    def other(hop):
        ox, oz, oc = (x + hop[0]) % 4, (z + hop[1]) % 2, (core + hop[2]) % 2
        return 4 * ox + 2 * oz + oc, 2 * ox + (oz + lat // deep) % 2, oc

    loads = [pltpu.make_async_copy(r.at[0], t, load_sem.at[i]) for i, (r, t) in enumerate(
        ((k_ref, raw.at[0]), (v_ref, raw.at[1]), (q_ref, send_qd.at[0]), (d_ref, send_qd.at[1])))]

    barrier = pltpu.get_barrier_semaphore()
    for hop in HOPS:
        pl.semaphore_signal(barrier, inc=1, device_id=(lat, other(hop)[0]), device_id_type=MESH)

    @pl.when(has_above)
    def _():
        pl.semaphore_signal(barrier, inc=1, device_id=above, device_id_type=MESH)

    @pl.when(has_below)
    def _():
        pl.semaphore_signal(barrier, inc=1, device_id=below, device_id_type=MESH)

    for load in loads:
        load.start()

    def kv_at(u, c):
        return either(c, 16 + STEP * u, 96 - STEP * u)

    def done_at(i):
        return by(either(core, TILE * i, COLS - TILE * i), TILE)

    def tile_of(i, c):
        return either(c, i, TILES - 1 - i)

    for i in range(2):
        loads[i].wait()
        for g in range(8):
            lanes = slice(g * LANES, (g + 1) * LANES)
            a = raw[i, :, lanes].astype(f32)
            a = jnp.concatenate([a[-SIDE:], a, a[:STEP - SIDE]], axis=0)
            shifted[i, :, lanes] = a.astype(bf16)
    loads[2].wait()
    loads[3].wait()

    pl.semaphore_wait(barrier, OTHERS + more_above + more_below)

    def kv_copy(u, g, c, first):
        off = either(c, 0, 96) if first else kv_at(u, c)
        size = 3 * TILE if first else STEP
        begin = (TILE * start_block(g, c) + off) % LON
        src = shifted.at[:, pl.ds(by(begin, TILE), size), pl.ds(by(g * LANES, LANES), LANES)]
        return src, got_kv.at[:, lon + RADIUS, pl.ds(by(off, TILE), size), :]

    def qd_copy(i, g, c):
        off = TILE * tile_of(i, c)
        begin = (TILE * start_block(g, c) + off) % LON
        src = send_qd.at[:, pl.ds(by(begin, TILE), TILE), pl.ds(by(g * LANES, LANES), LANES)]
        return src, got_qd.at[:, lon, pl.ds(by(off, TILE), TILE), :]

    def spread(pair, i, gone, came, own_sem):
        for hop in HOPS:
            to, g, c = other(hop)
            src, dst = pair(i, g, c)
            pltpu.make_async_remote_copy(src, dst, gone.at[i], came.at[i], device_id=(lat, to), device_id_type=MESH).start()
        src, dst = pair(i, group, core)
        pltpu.make_async_copy(src, dst, own_sem.at[i]).start()

    def spread_kv(u, first=False):
        spread(lambda i, g, c: kv_copy(i, g, c, first), u, sent_kv, came_kv, own_kv)

    def spread_qd(i):
        spread(qd_copy, i, sent_qd, came_qd, own_qd)

    spread_kv(0, True)

    @pl.loop(1, PARTS)
    def _(u):
        spread_kv(u)

        @pl.loop(2 * u - 2, 2 * u)
        def _(i):
            spread_qd(i)

    spread_qd(TILES - 2)
    spread_qd(TILES - 1)

    for half in range(2):
        mask[half] = window_mask(lat, lats, half)

    @pl.loop(0, TALL)
    def _(row):
        acc[:, row] = jnp.zeros((2, WIDE, LANES), f32)

    @pl.when(lat == 0)
    def _():
        got_kv[:, 0:RADIUS] = jnp.zeros((2, RADIUS, WIDE, LANES), bf16)

    @pl.when(lat == lats - 1)
    def _():
        got_kv[:, TALL - RADIUS:TALL] = jnp.zeros((2, RADIUS, WIDE, LANES), bf16)

    def came_wait(sem, u, ref, size):
        blank = ref.at[:, 0:OTHERS, 0:size, :]
        pltpu.make_async_copy(blank, blank, sem.at[u]).wait()

    def own_wait(sem, u, ref, size):
        blank = ref.at[:, 0, 0:size, :]
        pltpu.make_async_copy(blank, blank, sem.at[u]).wait()

    def relay(u, way, first):
        off = either(core, 0, 96) if first else kv_at(u, core)
        cols = pl.ds(by(off, TILE), 3 * TILE if first else STEP)
        here, there, to = ((slice(RADIUS, 2 * RADIUS), slice(TALL - RADIUS, TALL), above),
                           (slice(ROWS, ROWS + RADIUS), slice(0, RADIUS), below))[way]
        return pltpu.make_async_remote_copy(got_kv.at[:, here, cols, :], got_kv.at[:, there, cols, :], relay_out.at[u, way],
                                            relay_in.at[u, way], device_id=to, device_id_type=MESH)

    def edge(u, way):
        return pltpu.make_async_remote_copy(edge_out.at[u, way], edge_in.at[u, way], lat_out.at[u, way], lat_in.at[u, way],
                                            device_id=(above, below)[way], device_id_type=MESH)

    def last_edge(way):
        return pltpu.make_async_remote_copy(last_out.at[way], last_in.at[way], lat_out.at[TILES, way], lat_in.at[TILES, way],
                                            device_id=(above, below)[way], device_id_type=MESH)

    def side(i):
        return pltpu.make_async_remote_copy(side_out.at[i], side_in.at[i], side_gone.at[i], side_came.at[i],
                                            device_id=partner, device_id_type=MESH)

    out_lanes = pl.ds(by(group * LANES, LANES), LANES)

    def owner(i):
        return (start_block(group, core) + tile_of(i, core)) % DEVICES

    def q_pair(i):
        return final_q.at[i], out_ref.at[0, :, :, out_lanes]

    def kv_pair(i):
        return final_kv.at[i], out_ref.at[1:3, :, :, out_lanes]

    def hand_out(pair, i, gone, came):
        src, dst = pair(i)
        to = owner(i)

        @pl.when(to == lon)
        def _():
            pltpu.make_async_copy(src, dst, came.at[group]).start()

        @pl.when(to != lon)
        def _():
            pltpu.make_async_remote_copy(src, dst, gone.at[i], came.at[group], device_id=(lat, to), device_id_type=MESH).start()

    def hand_out_wait(pair, i, gone):
        src, dst = pair(i)
        to = owner(i)

        @pl.when(to != lon)
        def _():
            pltpu.make_async_remote_copy(src, dst, gone.at[i], gone.at[i], device_id=(lat, to), device_id_type=MESH).wait_send()

    own = slice(RADIUS, RADIUS + ROWS)

    def finish_kv(i):
        at = pl.ds(by(SIDE + TILE * tile_of(i, core), SIDE), TILE)
        final_kv[i] = acc[:, own, at].astype(bf16)

    def on_ways(make, then):
        @pl.when(has_above)
        def _():
            then(make(0))

        @pl.when(has_below)
        def _():
            then(make(1))

    def pass_keys(u):
        def go(first):
            size = 3 * TILE if first else STEP
            own_wait(own_kv, u, got_kv, size)
            came_wait(came_kv, u, got_kv, size)
            on_ways(lambda way: relay(u, way, first), lambda copy: copy.start())

        @pl.when(u == 0)
        def _():
            go(True)

        @pl.when(u > 0)
        def _():
            go(False)

    def relay_wait(u, way):
        @pl.when(u == 0)
        def _():
            relay(u, way, True).wait_recv()

        @pl.when(u > 0)
        def _():
            relay(u, way, False).wait_recv()

    last = by((1 - core) * COLS, TILE)

    def compute(i):
        begin = by(tile_of(i, core) * TILE, TILE)
        at, near = pl.ds(begin, TILE), pl.ds(begin, TWIDE)

        def half_tile(half):
            rows = slice(half * HALF, (half + 1) * HALF)
            spans = slice(half * HALF, half * HALF + SPAN)
            q = got_qd[0, rows, at].reshape(HALF * TILE, LANES)
            d = got_qd[1, rows, at].reshape(HALF * TILE, LANES)
            k = got_kv[0, spans, near].reshape(SPAN * TWIDE, LANES)
            v = got_kv[1, spans, near].reshape(SPAN * TWIDE, LANES)
            dq, dk, dv = pair_grads(q, d, k, v, mask[half])
            final_q[i, rows] = dq.astype(bf16).reshape(HALF, TILE, LANES)
            acc[0, spans, near] += dk.reshape(SPAN, TWIDE, LANES)
            acc[1, spans, near] += dv.reshape(SPAN, TWIDE, LANES)

        def send_edge(way):
            rows = (slice(0, RADIUS), slice(TALL - RADIUS, TALL))[way]
            edge_out[i, way] = acc[:, rows, pl.ds(done_at(i), TILE)].astype(bf16)
            edge(i, way).start()

            @pl.when(i == TILES - 1)
            def _():
                last_out[way] = acc[:, rows, pl.ds(last, TILE)].astype(bf16)
                last_edge(way).start()

        @pl.when((i % 2 == 0) & has_above)
        def _():
            relay_wait(i // 2, 1)

        half_tile(0)

        @pl.when(has_above)
        def _():
            send_edge(0)

        @pl.when((i % 2 == 0) & has_below)
        def _():
            relay_wait(i // 2, 0)

        half_tile(1)

        @pl.when(has_below)
        def _():
            send_edge(1)

    def add_edges(i):
        def add(way):
            rows = (slice(ROWS, ROWS + RADIUS), slice(RADIUS, 2 * RADIUS))[way]
            edge(i, way).wait_recv()
            acc[:, rows, pl.ds(done_at(i), TILE)] += edge_in[i, way].astype(f32)

            @pl.when(i == TILES - 1)
            def _():
                last_edge(way).wait_recv()
                acc[:, rows, pl.ds(last, TILE)] += last_in[way].astype(f32)

        @pl.when(has_below)
        def _():
            add(0)

        @pl.when(has_above)
        def _():
            add(1)

        def send_side(n, at):
            cols = pl.ds(by(at, SIDE), SIDE)
            side_out[n] = jnp.concatenate([acc[0, own, cols], acc[1, own, cols]], axis=1).astype(bf16)
            side(n).start()

        @pl.when(i == 0)
        def _():
            send_side(0, core * (WIDE - SIDE))

        @pl.when(i == TILES - 1)
        def _():
            send_side(1, (1 - core) * (WIDE - SIDE))

    def add_side(n, at):
        side(n).wait_recv()
        cols = pl.ds(by(at, SIDE), SIDE)
        got = side_in[n].astype(f32)
        acc[0, own, cols] += got[:, :SIDE]
        acc[1, own, cols] += got[:, SIDE:]

    @pl.loop(0, TILES)
    def _(i):
        @pl.when(i == 0)
        def _():
            pass_keys(0)

        @pl.when((i % 2 == 0) & (i < TILES - 2))
        def _():
            pass_keys(i // 2 + 1)

        own_wait(own_qd, i, got_qd, TILE)
        came_wait(came_qd, i, got_qd, TILE)

        compute(i)
        hand_out(q_pair, i, q_gone, q_came)

        @pl.when(i > 1)
        def _():
            add_edges(i - 2)

        @pl.when(i == 3)
        def _():
            add_side(0, either(core, SIDE, COLS))

        @pl.when(i > 2)
        def _():
            finish_kv(i - 3)
            hand_out(kv_pair, i - 3, kv_gone, kv_came)

    add_edges(TILES - 2)
    finish_kv(TILES - 3)
    hand_out(kv_pair, TILES - 3, kv_gone, kv_came)
    add_edges(TILES - 1)
    finish_kv(TILES - 2)
    hand_out(kv_pair, TILES - 2, kv_gone, kv_came)
    add_side(1, either(core, COLS, SIDE))
    finish_kv(TILES - 1)
    hand_out(kv_pair, TILES - 1, kv_gone, kv_came)

    came_wait(sent_kv, 0, got_kv, 3 * TILE)
    on_ways(lambda way: relay(0, way, True), lambda copy: copy.wait_send())

    @pl.loop(1, PARTS)
    def _(u):
        came_wait(sent_kv, u, got_kv, STEP)
        on_ways(lambda way: relay(u, way, False), lambda copy: copy.wait_send())

    on_ways(last_edge, lambda copy: copy.wait_send())
    side(0).wait_send()
    side(1).wait_send()

    @pl.loop(0, TILES)
    def _(i):
        came_wait(sent_qd, i, got_qd, TILE)
        on_ways(lambda way: edge(i, way), lambda copy: copy.wait_send())
        hand_out_wait(q_pair, i, q_gone)
        hand_out_wait(kv_pair, i, kv_gone)
        for pair, came in ((q_pair, q_came), (kv_pair, kv_came)):
            src, dst = pair(i)
            pltpu.make_async_copy(src, dst, came.at[i]).wait()


def part_kernel(all_ref, *refs):
    outs, (held, load_sem, store_sem) = refs[:3], refs[3:]
    size = ROWS // PIECES
    pairs = [(i, j, slice(j * size, (j + 1) * size)) for i in range(3) for j in range(PIECES)]
    loads = [pltpu.make_async_copy(all_ref.at[i, s], held.at[i, s], load_sem.at[i, j]) for i, j, s in pairs]
    stores = [pltpu.make_async_copy(held.at[i, s], outs[i].at[s], store_sem.at[i, j]) for i, j, s in pairs]
    for load in loads:
        load.start()
    for load, store in zip(loads, stores):
        load.wait()
        store.start()
    for store in stores:
        store.wait()


def on_device(queries, keys, values, grads_out):
    lats = lax.axis_size("lat")
    features = queries.shape[-1]
    vmem = lambda *shape: pltpu.VMEM(shape, bf16)
    sems = lambda *shape: pltpu.SemaphoreType.DMA(shape)
    out = pl.pallas_call(
        functools.partial(kernel, lats),
        out_shape=jax.ShapeDtypeStruct((3, ROWS, TILE, features), bf16),
        in_specs=[pl.BlockSpec(memory_space=pl.ANY)] * 4,
        out_specs=pl.BlockSpec(memory_space=pl.ANY),
        scratch_shapes=[
            vmem(2, LON, features),
            vmem(2, LON + STEP, features),
            vmem(2, LON, features),
            vmem(2, TALL, WIDE, LANES),
            vmem(2, ROWS, COLS, LANES),
            pltpu.VMEM((2, SPAN * TWIDE, 2 * HALF * TILE), f32),
            pltpu.VMEM((2, TALL, WIDE, LANES), f32),
            vmem(TILES, 2, 2, RADIUS, TILE, LANES),
            vmem(TILES, 2, 2, RADIUS, TILE, LANES),
            vmem(2, 2, RADIUS, TILE, LANES),
            vmem(2, 2, RADIUS, TILE, LANES),
            vmem(2, ROWS, 2 * SIDE, LANES),
            vmem(2, ROWS, 2 * SIDE, LANES),
            vmem(TILES, ROWS, TILE, LANES),
            vmem(TILES, 2, ROWS, TILE, LANES),
            sems(4), sems(PARTS), sems(TILES), sems(PARTS), sems(TILES), sems(PARTS), sems(TILES),
            sems(PARTS, 2), sems(PARTS, 2), sems(TILES + 1, 2), sems(TILES + 1, 2), sems(2), sems(2),
            sems(TILES), sems(TILES), sems(TILES), sems(TILES),
        ],
        compiler_params=pltpu.CompilerParams(collective_id=0, has_side_effects=True, vmem_limit_bytes=56 * 1024 * 1024),
    )(queries, keys, values, grads_out)
    shape = jax.ShapeDtypeStruct(out.shape[1:], bf16)
    return pl.pallas_call(
        part_kernel,
        in_specs=[pl.BlockSpec(memory_space=pl.ANY)],
        out_specs=[pl.BlockSpec(memory_space=pl.ANY)] * 3,
        out_shape=[shape] * 3,
        scratch_shapes=[pltpu.VMEM(out.shape, bf16), sems(3, PIECES), sems(3, PIECES)],
    )(out)


def solution(mesh):
    placed = P(("lat", "lon"), None, None)
    return jax.shard_map(
        on_device,
        mesh=mesh,
        in_specs=(placed,) * 4,
        out_specs=(P("lat", "lon", None),) * 3,
        check_vma=False,
    )
```

```python
import functools

import jax
import jax.numpy as jnp
from jax import lax
from jax.experimental import pallas as pl
from jax.experimental.pallas import tpu as pltpu
from jax.sharding import PartitionSpec as P

HEAD = 64
LANES = 128
RADIUS = 6
SIDE = 8
LON = 256
ROWS = 16
TILE = 16
TILES = 8
PIECES = 4
PARTS = 4
STEP = 2 * TILE
COLS = TILES * TILE
WIDE = COLS + 2 * SIDE
TALL = ROWS + 2 * RADIUS
HALF = ROWS // 2
SPAN = HALF + 2 * RADIUS
TWIDE = TILE + 2 * SIDE
DEVICES = 16
OTHERS = DEVICES - 1

MESH = pl.DeviceIdType.MESH
bf16 = jnp.bfloat16
f32 = jnp.float32
masked_score = -1e30


def dot(a, b, ca, cb):
    return lax.dot_general(a, b, (((ca,), (cb,)), ((), ())), preferred_element_type=f32)


def window_mask(lat, lats, half):
    shape = (SPAN * TWIDE, HALF * TILE)
    key = lax.broadcasted_iota(jnp.int32, shape, 0)
    query = lax.broadcasted_iota(jnp.int32, shape, 1)
    down = key // TWIDE - query // TILE
    right = key % TWIDE - query % TILE
    row = lat * ROWS - RADIUS + half * HALF + key // TWIDE
    ok = (down >= 0) & (down <= 2 * RADIUS)
    ok &= (right >= SIDE - RADIUS) & (right <= SIDE + RADIUS)
    ok &= (row >= 0) & (row < lats * ROWS)
    ok = jnp.where(ok, 0.0, masked_score)
    return jnp.concatenate([ok, ok], axis=1)


def pair_grads(q, d, k, v, mask):
    first = lax.broadcasted_iota(jnp.int32, q.shape, 1) < HEAD
    zero = jnp.zeros_like(q)
    q = q * (HEAD ** -0.5)
    q2 = jnp.concatenate([jnp.where(first, q, zero), jnp.where(first, zero, q)], axis=0)
    d2 = jnp.concatenate([jnp.where(first, d, zero), jnp.where(first, zero, d)], axis=0)
    s = dot(k, q2, 1, 1) + mask
    e = jnp.exp(s - jnp.max(s, axis=0, keepdims=True))
    p = e * (1.0 / jnp.sum(e, axis=0, keepdims=True))
    dp = dot(v, d2, 1, 1)
    centre = jnp.sum(p * dp, axis=0, keepdims=True)
    ds = (p * (dp - centre)).astype(bf16)
    dv = dot(p.astype(bf16), d2, 1, 0)
    dk = dot(ds, q2, 1, 0)
    dq = dot(ds, k, 0, 0) * (HEAD ** -0.5)
    count = q.shape[0]
    return jnp.where(first, dq[:count], dq[count:]), dk, dv


HOPS = [(1, 0, 0), (3, 0, 0), (0, 1, 0), (2, 0, 0), (1, 1, 0), (3, 1, 0), (0, 1, 1), (2, 1, 0), (1, 0, 1),
        (3, 0, 1), (2, 0, 1), (1, 1, 1), (3, 1, 1), (2, 1, 1), (0, 0, 1)]


def either(core, a, b):
    return (1 - core) * a + core * b


def by(value, unit):
    return pl.multiple_of(value, unit)


def kernel(lats, q_ref, k_ref, v_ref, d_ref, out_ref, raw, shifted, send_qd, got_kv, got_qd, mask, acc, edge_out, edge_in,
           last_out, last_in, side_out, side_in, final_q, final_kv, load_sem, sent_kv, sent_qd, came_kv, came_qd, own_kv, own_qd,
           relay_out, relay_in, lat_out, lat_in, side_gone, side_came, q_gone, q_came, kv_gone, kv_came):
    lat, lon = lax.axis_index("lat"), lax.axis_index("lon")
    x, z, core = lon // 4, (lon // 2) % 2, lon % 2
    deep = lats // 2
    group = 2 * x + (z + lat // deep) % 2
    partner = (lat, lon + 1 - 2 * core)
    has_above, has_below = lat > 0, lat < lats - 1
    more_above, more_below = (lat + lats - 1) // lats, (2 * lats - 2 - lat) // lats

    def neighbour(other_lat):
        return other_lat, 4 * x + 2 * ((z + lat // deep + other_lat // deep) % 2) + core

    above, below = neighbour(lat - more_above), neighbour(lat + more_below)

    def start_block(g, c):
        return (2 * g + 10 + (DEVICES // 2) * c) % DEVICES

    def other(hop):
        ox, oz, oc = (x + hop[0]) % 4, (z + hop[1]) % 2, (core + hop[2]) % 2
        return 4 * ox + 2 * oz + oc, 2 * ox + (oz + lat // deep) % 2, oc

    loads = [pltpu.make_async_copy(r.at[0], t, load_sem.at[i]) for i, (r, t) in enumerate(
        ((k_ref, raw.at[0]), (v_ref, raw.at[1]), (q_ref, send_qd.at[0]), (d_ref, send_qd.at[1])))]

    barrier = pltpu.get_barrier_semaphore()
    for hop in HOPS:
        pl.semaphore_signal(barrier, inc=1, device_id=(lat, other(hop)[0]), device_id_type=MESH)

    @pl.when(has_above)
    def _():
        pl.semaphore_signal(barrier, inc=1, device_id=above, device_id_type=MESH)

    @pl.when(has_below)
    def _():
        pl.semaphore_signal(barrier, inc=1, device_id=below, device_id_type=MESH)

    for load in loads:
        load.start()

    def kv_at(u, c):
        return either(c, 16 + STEP * u, 96 - STEP * u)

    def done_at(i):
        return by(either(core, TILE * i, COLS - TILE * i), TILE)

    def tile_of(i, c):
        return either(c, i, TILES - 1 - i)

    for i in range(2):
        loads[i].wait()
        for g in range(8):
            lanes = slice(g * LANES, (g + 1) * LANES)
            a = raw[i, :, lanes].astype(f32)
            a = jnp.concatenate([a[-SIDE:], a, a[:STEP - SIDE]], axis=0)
            shifted[i, :, lanes] = a.astype(bf16)

    pl.semaphore_wait(barrier, OTHERS + more_above + more_below)

    def kv_copy(u, g, c, first):
        off = either(c, 0, 96) if first else kv_at(u, c)
        size = 3 * TILE if first else STEP
        begin = (TILE * start_block(g, c) + off) % LON
        src = shifted.at[:, pl.ds(by(begin, TILE), size), pl.ds(by(g * LANES, LANES), LANES)]
        return src, got_kv.at[:, lon + RADIUS, pl.ds(by(off, TILE), size), :]

    def qd_copy(i, g, c):
        off = TILE * tile_of(i, c)
        begin = (TILE * start_block(g, c) + off) % LON
        src = send_qd.at[:, pl.ds(by(begin, TILE), TILE), pl.ds(by(g * LANES, LANES), LANES)]
        return src, got_qd.at[:, lon, pl.ds(by(off, TILE), TILE), :]

    def spread(pair, i, gone, came, own_sem):
        for hop in HOPS:
            to, g, c = other(hop)
            src, dst = pair(i, g, c)
            pltpu.make_async_remote_copy(src, dst, gone.at[i], came.at[i], device_id=(lat, to), device_id_type=MESH).start()
        src, dst = pair(i, group, core)
        pltpu.make_async_copy(src, dst, own_sem.at[i]).start()

    def spread_kv(u, first=False):
        spread(lambda i, g, c: kv_copy(i, g, c, first), u, sent_kv, came_kv, own_kv)

    def spread_qd(i):
        spread(qd_copy, i, sent_qd, came_qd, own_qd)

    spread_kv(0, True)
    spread_kv(1)
    loads[2].wait()
    loads[3].wait()
    spread_qd(0)
    spread_qd(1)

    @pl.loop(2, PARTS)
    def _(u):
        spread_kv(u)

        @pl.loop(2 * u - 2, 2 * u)
        def _(i):
            spread_qd(i)

    spread_qd(TILES - 2)
    spread_qd(TILES - 1)

    for half in range(2):
        mask[half] = window_mask(lat, lats, half)

    @pl.loop(0, TALL)
    def _(row):
        acc[:, row] = jnp.zeros((2, WIDE, LANES), f32)

    @pl.when(lat == 0)
    def _():
        got_kv[:, 0:RADIUS] = jnp.zeros((2, RADIUS, WIDE, LANES), bf16)

    @pl.when(lat == lats - 1)
    def _():
        got_kv[:, TALL - RADIUS:TALL] = jnp.zeros((2, RADIUS, WIDE, LANES), bf16)

    def came_wait(sem, u, ref, size):
        blank = ref.at[:, 0:OTHERS, 0:size, :]
        pltpu.make_async_copy(blank, blank, sem.at[u]).wait()

    def own_wait(sem, u, ref, size):
        blank = ref.at[:, 0, 0:size, :]
        pltpu.make_async_copy(blank, blank, sem.at[u]).wait()

    def relay(u, way, first):
        off = either(core, 0, 96) if first else kv_at(u, core)
        cols = pl.ds(by(off, TILE), 3 * TILE if first else STEP)
        here, there, to = ((slice(RADIUS, 2 * RADIUS), slice(TALL - RADIUS, TALL), above),
                           (slice(ROWS, ROWS + RADIUS), slice(0, RADIUS), below))[way]
        return pltpu.make_async_remote_copy(got_kv.at[:, here, cols, :], got_kv.at[:, there, cols, :], relay_out.at[u, way],
                                            relay_in.at[u, way], device_id=to, device_id_type=MESH)

    def edge(u, way):
        return pltpu.make_async_remote_copy(edge_out.at[u, way], edge_in.at[u, way], lat_out.at[u, way], lat_in.at[u, way],
                                            device_id=(above, below)[way], device_id_type=MESH)

    def last_edge(way):
        return pltpu.make_async_remote_copy(last_out.at[way], last_in.at[way], lat_out.at[TILES, way], lat_in.at[TILES, way],
                                            device_id=(above, below)[way], device_id_type=MESH)

    def side(i):
        return pltpu.make_async_remote_copy(side_out.at[i], side_in.at[i], side_gone.at[i], side_came.at[i],
                                            device_id=partner, device_id_type=MESH)

    out_lanes = pl.ds(by(group * LANES, LANES), LANES)

    def owner(i):
        return (start_block(group, core) + tile_of(i, core)) % DEVICES

    def q_pair(i):
        return final_q.at[i], out_ref.at[0, :, :, out_lanes]

    def kv_pair(i):
        return final_kv.at[i], out_ref.at[1:3, :, :, out_lanes]

    def hand_out(pair, i, gone, came):
        src, dst = pair(i)
        to = owner(i)

        @pl.when(to == lon)
        def _():
            pltpu.make_async_copy(src, dst, came.at[group]).start()

        @pl.when(to != lon)
        def _():
            pltpu.make_async_remote_copy(src, dst, gone.at[i], came.at[group], device_id=(lat, to), device_id_type=MESH).start()

    def hand_out_wait(pair, i, gone):
        src, dst = pair(i)
        to = owner(i)

        @pl.when(to != lon)
        def _():
            pltpu.make_async_remote_copy(src, dst, gone.at[i], gone.at[i], device_id=(lat, to), device_id_type=MESH).wait_send()

    own = slice(RADIUS, RADIUS + ROWS)

    def finish_kv(i):
        at = pl.ds(by(SIDE + TILE * tile_of(i, core), SIDE), TILE)
        final_kv[i] = acc[:, own, at].astype(bf16)

    def on_ways(make, then):
        @pl.when(has_above)
        def _():
            then(make(0))

        @pl.when(has_below)
        def _():
            then(make(1))

    def pass_keys(u):
        def go(first):
            size = 3 * TILE if first else STEP
            own_wait(own_kv, u, got_kv, size)
            came_wait(came_kv, u, got_kv, size)
            on_ways(lambda way: relay(u, way, first), lambda copy: copy.start())

        @pl.when(u == 0)
        def _():
            go(True)

        @pl.when(u > 0)
        def _():
            go(False)

    def relay_wait(u, way):
        @pl.when(u == 0)
        def _():
            relay(u, way, True).wait_recv()

        @pl.when(u > 0)
        def _():
            relay(u, way, False).wait_recv()

    last = by((1 - core) * COLS, TILE)

    def compute(i):
        begin = by(tile_of(i, core) * TILE, TILE)
        at, near = pl.ds(begin, TILE), pl.ds(begin, TWIDE)

        def half_tile(half):
            rows = slice(half * HALF, (half + 1) * HALF)
            spans = slice(half * HALF, half * HALF + SPAN)
            q = got_qd[0, rows, at].reshape(HALF * TILE, LANES)
            d = got_qd[1, rows, at].reshape(HALF * TILE, LANES)
            k = got_kv[0, spans, near].reshape(SPAN * TWIDE, LANES)
            v = got_kv[1, spans, near].reshape(SPAN * TWIDE, LANES)
            dq, dk, dv = pair_grads(q, d, k, v, mask[half])
            final_q[i, rows] = dq.astype(bf16).reshape(HALF, TILE, LANES)
            acc[0, spans, near] += dk.reshape(SPAN, TWIDE, LANES)
            acc[1, spans, near] += dv.reshape(SPAN, TWIDE, LANES)

        def send_edge(way):
            rows = (slice(0, RADIUS), slice(TALL - RADIUS, TALL))[way]
            edge_out[i, way] = acc[:, rows, pl.ds(done_at(i), TILE)].astype(bf16)
            edge(i, way).start()

            @pl.when(i == TILES - 1)
            def _():
                last_out[way] = acc[:, rows, pl.ds(last, TILE)].astype(bf16)
                last_edge(way).start()

        @pl.when((i % 2 == 0) & has_above)
        def _():
            relay_wait(i // 2, 1)

        half_tile(0)

        @pl.when(has_above)
        def _():
            send_edge(0)

        @pl.when((i % 2 == 0) & has_below)
        def _():
            relay_wait(i // 2, 0)

        half_tile(1)

        @pl.when(has_below)
        def _():
            send_edge(1)

    def add_edges(i):
        def add(way):
            rows = (slice(ROWS, ROWS + RADIUS), slice(RADIUS, 2 * RADIUS))[way]
            edge(i, way).wait_recv()
            acc[:, rows, pl.ds(done_at(i), TILE)] += edge_in[i, way].astype(f32)

            @pl.when(i == TILES - 1)
            def _():
                last_edge(way).wait_recv()
                acc[:, rows, pl.ds(last, TILE)] += last_in[way].astype(f32)

        @pl.when(has_below)
        def _():
            add(0)

        @pl.when(has_above)
        def _():
            add(1)

        def send_side(n, at):
            cols = pl.ds(by(at, SIDE), SIDE)
            side_out[n] = jnp.concatenate([acc[0, own, cols], acc[1, own, cols]], axis=1).astype(bf16)
            side(n).start()

        @pl.when(i == 0)
        def _():
            send_side(0, core * (WIDE - SIDE))

        @pl.when(i == TILES - 1)
        def _():
            send_side(1, (1 - core) * (WIDE - SIDE))

    def add_side(n, at):
        side(n).wait_recv()
        cols = pl.ds(by(at, SIDE), SIDE)
        got = side_in[n].astype(f32)
        acc[0, own, cols] += got[:, :SIDE]
        acc[1, own, cols] += got[:, SIDE:]

    @pl.loop(0, TILES)
    def _(i):
        @pl.when(i == 0)
        def _():
            pass_keys(0)

        @pl.when((i % 2 == 0) & (i < TILES - 2))
        def _():
            pass_keys(i // 2 + 1)

        own_wait(own_qd, i, got_qd, TILE)
        came_wait(came_qd, i, got_qd, TILE)

        compute(i)
        hand_out(q_pair, i, q_gone, q_came)

        @pl.when(i > 1)
        def _():
            add_edges(i - 2)

        @pl.when(i == 3)
        def _():
            add_side(0, either(core, SIDE, COLS))

        @pl.when(i > 2)
        def _():
            finish_kv(i - 3)
            hand_out(kv_pair, i - 3, kv_gone, kv_came)

    add_edges(TILES - 2)
    finish_kv(TILES - 3)
    hand_out(kv_pair, TILES - 3, kv_gone, kv_came)
    add_edges(TILES - 1)
    finish_kv(TILES - 2)
    hand_out(kv_pair, TILES - 2, kv_gone, kv_came)
    add_side(1, either(core, COLS, SIDE))
    finish_kv(TILES - 1)
    hand_out(kv_pair, TILES - 1, kv_gone, kv_came)

    came_wait(sent_kv, 0, got_kv, 3 * TILE)
    on_ways(lambda way: relay(0, way, True), lambda copy: copy.wait_send())

    @pl.loop(1, PARTS)
    def _(u):
        came_wait(sent_kv, u, got_kv, STEP)
        on_ways(lambda way: relay(u, way, False), lambda copy: copy.wait_send())

    on_ways(last_edge, lambda copy: copy.wait_send())
    side(0).wait_send()
    side(1).wait_send()

    @pl.loop(0, TILES)
    def _(i):
        came_wait(sent_qd, i, got_qd, TILE)
        on_ways(lambda way: edge(i, way), lambda copy: copy.wait_send())
        hand_out_wait(q_pair, i, q_gone)
        hand_out_wait(kv_pair, i, kv_gone)
        for pair, came in ((q_pair, q_came), (kv_pair, kv_came)):
            src, dst = pair(i)
            pltpu.make_async_copy(src, dst, came.at[i]).wait()


def part_kernel(all_ref, *refs):
    outs, (held, load_sem, store_sem) = refs[:3], refs[3:]
    size = ROWS // PIECES
    pairs = [(i, j, slice(j * size, (j + 1) * size)) for i in range(3) for j in range(PIECES)]
    loads = [pltpu.make_async_copy(all_ref.at[i, s], held.at[i, s], load_sem.at[i, j]) for i, j, s in pairs]
    stores = [pltpu.make_async_copy(held.at[i, s], outs[i].at[s], store_sem.at[i, j]) for i, j, s in pairs]
    for load in loads:
        load.start()
    for load, store in zip(loads, stores):
        load.wait()
        store.start()
    for store in stores:
        store.wait()


def on_device(queries, keys, values, grads_out):
    lats = lax.axis_size("lat")
    features = queries.shape[-1]
    vmem = lambda *shape: pltpu.VMEM(shape, bf16)
    sems = lambda *shape: pltpu.SemaphoreType.DMA(shape)
    out = pl.pallas_call(
        functools.partial(kernel, lats),
        out_shape=jax.ShapeDtypeStruct((3, ROWS, TILE, features), bf16),
        in_specs=[pl.BlockSpec(memory_space=pl.ANY)] * 4,
        out_specs=pl.BlockSpec(memory_space=pl.ANY),
        scratch_shapes=[
            vmem(2, LON, features),
            vmem(2, LON + STEP, features),
            vmem(2, LON, features),
            vmem(2, TALL, WIDE, LANES),
            vmem(2, ROWS, COLS, LANES),
            pltpu.VMEM((2, SPAN * TWIDE, 2 * HALF * TILE), f32),
            pltpu.VMEM((2, TALL, WIDE, LANES), f32),
            vmem(TILES, 2, 2, RADIUS, TILE, LANES),
            vmem(TILES, 2, 2, RADIUS, TILE, LANES),
            vmem(2, 2, RADIUS, TILE, LANES),
            vmem(2, 2, RADIUS, TILE, LANES),
            vmem(2, ROWS, 2 * SIDE, LANES),
            vmem(2, ROWS, 2 * SIDE, LANES),
            vmem(TILES, ROWS, TILE, LANES),
            vmem(TILES, 2, ROWS, TILE, LANES),
            sems(4), sems(PARTS), sems(TILES), sems(PARTS), sems(TILES), sems(PARTS), sems(TILES),
            sems(PARTS, 2), sems(PARTS, 2), sems(TILES + 1, 2), sems(TILES + 1, 2), sems(2), sems(2),
            sems(TILES), sems(TILES), sems(TILES), sems(TILES),
        ],
        compiler_params=pltpu.CompilerParams(collective_id=0, has_side_effects=True, vmem_limit_bytes=56 * 1024 * 1024),
    )(queries, keys, values, grads_out)
    shape = jax.ShapeDtypeStruct(out.shape[1:], bf16)
    return pl.pallas_call(
        part_kernel,
        in_specs=[pl.BlockSpec(memory_space=pl.ANY)],
        out_specs=[pl.BlockSpec(memory_space=pl.ANY)] * 3,
        out_shape=[shape] * 3,
        scratch_shapes=[pltpu.VMEM(out.shape, bf16), sems(3, PIECES), sems(3, PIECES)],
    )(out)


def solution(mesh):
    placed = P(("lat", "lon"), None, None)
    return jax.shard_map(
        on_device,
        mesh=mesh,
        in_specs=(placed,) * 4,
        out_specs=(P("lat", "lon", None),) * 3,
        check_vma=False,
    )
```
